128 devices in a mesh: sec: 8 (over x_hi, z), tile: 16 (over y, x_lo, core).
Axes of the slice: x: 4 (x_hi: 2, x_lo: 2; x = x_hi * 2 + x_lo), y: 4, z: 4, core: 2. Of those that a mesh axis runs over, the one named last changes fastest.
Arguments:
- sections: float32 [8, 2048, 8192], P('sec', 'tile'), may hold values from -12 to 12
- masks: int32 [8, 32, 128], P('sec', 'tile'), may hold values 0 or 1
- carried: float32 [2, 32, 128], P(None, 'tile'), may hold values from -8 to 8
Outputs:
- flow: float32 [8, 2, 32, 128], P('sec', None, 'tile')
- aligned: float32 [8, 2, 32, 128], P('sec', None, 'tile')
The draws below stay inside these ranges and needn't reach their ends.
All inputs are finite; a program needn't handle non-finite values. No bound on the sum of `masks` on one device may be relied on, other than what follows from the above.
Results may differ from the reference program's by a relative error of at most 0.000098.
Values sent between devices are 32-bit elements; how exact they have to be, the bound alone decides.
A program may use at most 128 MiB of HBM per device.

```python
import math
import jax
import jax.numpy as jnp
from jax import lax

COLS = 8192
PATCH = 128
STRIDE = 64
ITERS = 3
SECTIONS = 8
ROWS = 2048
NODE_ROWS = 32
NODE_COLS = 128


def draw_sections(key, part):
    key = jax.random.fold_in(key, 7)
    keys = jax.random.split(key, 4)
    field = jax.random.normal(keys[0], (ROWS, COLS), jnp.float32)
    field = (field + jnp.roll(field, 1, 0) + jnp.roll(field, 1, 1)) / math.sqrt(3.0)
    moves = jax.random.randint(keys[1], (SECTIONS, 2), -6, 7)

    def placed(move):
        return jnp.roll(jnp.roll(field, move[0], 0), move[1], 1)
    moved = jax.vmap(placed)(moves)
    noise = jax.random.normal(keys[3], (SECTIONS, ROWS, COLS), jnp.float32)
    gains = jax.random.uniform(keys[2], (SECTIONS, ROWS // STRIDE, COLS // STRIDE), jnp.float32, 0.0, 0.6)
    gains = jnp.repeat(jnp.repeat(gains, STRIDE, 1), STRIDE, 2)
    return jnp.clip(gains * moved + noise, -12.0, 12.0)


def set_ends(entries, stream_key, low, high):
    shape = entries.shape
    place = [jax.random.randint(jax.random.fold_in(stream_key, axis), (), 0, shape[axis]) for axis in range(len(shape))]
    entries = entries.at[tuple(place)].set(low)
    longest = shape.index(max(shape))
    place[longest] = (place[longest] + 1) % shape[longest]
    return entries.at[tuple(place)].set(high)


def shard_levels(own_key, extent, pieces, low, top_value):
    def one(axis_at, parts):
        draws = jax.random.uniform(jax.random.fold_in(jax.random.fold_in(own_key, 6), axis_at), (parts,), jnp.float32, low / len(pieces), top_value / len(pieces))
        return jnp.repeat(jnp.exp(draws), extent[axis_at] // parts).reshape((-1,) + (1,) * (len(extent) - axis_at - 1))

    factor_of = one(*pieces[0])
    for cut in pieces[1:]:
        factor_of = factor_of * one(*cut)
    return factor_of


def bell_draw(key, dims, scale, most, shards=(), kind=jnp.bfloat16):
    array = jax.random.normal(key, dims, jnp.float32) * scale
    if len(shards) > 0:
        array = shard_levels(key, dims, shards, -0.22, 0.18) * array
    return jnp.clip(array, min=-most, max=most).astype(kind)


def setup_inputs(seed: int = 0) -> dict:
    streams_of = jax.random.split(jax.random.key(seed), 4)
    return {
        "sections": draw_sections(jax.random.fold_in(streams_of[3], 71), 0),
        "masks": set_ends((jax.random.randint(streams_of[1], (SECTIONS, NODE_ROWS, NODE_COLS), 0, 4) < 3).astype(jnp.int32), jax.random.fold_in(streams_of[1], 1), 0, 1),
        "carried": bell_draw(streams_of[2], (2, NODE_ROWS, NODE_COLS), 2.0, 8.0, ((1, 16),), jnp.float32),
    }


spring_weight = 1.0
link_weight = 4.0
anchor_weight = 0.5


def band_patches(band):
    columns = COLS // STRIDE
    cells = band.reshape(PATCH, columns + 1, STRIDE)
    joined = jnp.concatenate([cells[:, :-1], cells[:, 1:]], axis=2)
    return joined.transpose(1, 0, 2)


def pair_flow(earlier, later):
    wrapped = ((jnp.arange(PATCH) + PATCH // 2) % PATCH - PATCH // 2).astype(jnp.float32)

    def node_row(index):
        first = lax.dynamic_slice_in_dim(earlier, index * STRIDE, PATCH, 0)
        second = lax.dynamic_slice_in_dim(later, index * STRIDE, PATCH, 0)
        spec = jnp.conj(jnp.fft.fft2(band_patches(first))) * jnp.fft.fft2(band_patches(second))
        corr = jnp.real(jnp.fft.ifft2(spec)).astype(jnp.float32)
        scores = corr / PATCH
        count = scores.shape[0]
        weights = jax.nn.softmax(scores.reshape(count, -1), axis=-1).reshape(count, PATCH, PATCH)
        along_rows = jnp.sum(weights * wrapped[None, :, None], axis=(1, 2))
        along_cols = jnp.sum(weights * wrapped[None, None, :], axis=(1, 2))
        return jnp.stack([along_rows, along_cols])

    result = lax.map(node_row, jnp.arange(NODE_ROWS, dtype=jnp.int32))
    return result.transpose(1, 0, 2)


def reference(sections, masks, carried):
    padded = jnp.pad(sections, ((0, 0), (0, STRIDE), (0, STRIDE)))
    rest = lax.map(lambda s: pair_flow(padded[s - 1], padded[s]), jnp.arange(1, SECTIONS, dtype=jnp.int32))
    flow = jnp.concatenate([carried[None].astype(jnp.float32), rest], axis=0)
    later_sec = (jnp.arange(SECTIONS) > 0).astype(jnp.float32)
    pairs = masks.astype(jnp.float32) * later_sec[:, None, None]
    start = jnp.cumsum(flow, axis=0)
    next_flow = jnp.concatenate([flow[1:], jnp.zeros_like(flow[:1])], axis=0)
    next_pair = jnp.concatenate([pairs[1:], jnp.zeros_like(pairs[:1])], axis=0)
    rows = jnp.arange(NODE_ROWS)
    cols = jnp.arange(NODE_COLS)
    degree = (4.0 - (rows == 0).astype(jnp.float32)[:, None] - (rows == NODE_ROWS - 1).astype(jnp.float32)[:, None]
              - (cols == 0).astype(jnp.float32)[None, :] - (cols == NODE_COLS - 1).astype(jnp.float32)[None, :])
    denom = spring_weight * degree[None] + link_weight * pairs + link_weight * next_pair + anchor_weight
    aligned = start
    for step in range(ITERS):
        grid = jnp.pad(aligned, ((1, 1), (0, 0), (1, 1), (1, 1)))
        beside = (grid[1:-1, :, :-2, 1:-1] + grid[1:-1, :, 2:, 1:-1]
                  + grid[1:-1, :, 1:-1, :-2] + grid[1:-1, :, 1:-1, 2:])
        before = grid[:-2, :, 1:-1, 1:-1]
        after = grid[2:, :, 1:-1, 1:-1]
        total = (spring_weight * beside + link_weight * pairs[:, None] * (before + flow)
                 + link_weight * next_pair[:, None] * (after - next_flow) + anchor_weight * start)
        aligned = total / denom[:, None]
    return flow, aligned
```

```python
import functools
import math

import jax
import jax.numpy as jnp
import ml_dtypes
import numpy as np
from jax import lax
from jax.experimental import pallas as pl
from jax.experimental.pallas import tpu as pltpu
from jax.sharding import PartitionSpec as P

COLS = 8192
PATCH = 128
STRIDE = 64
ITERS = 3
HALF = PATCH // 2
TILES = 8
QUAD = 4
SIDE = 33

spring_weight = 1.0
link_weight = 4.0
anchor_weight = 0.5
bf16 = jnp.bfloat16
f32 = jnp.float32


def two_terms(table):
    table = table.astype(np.float32)
    high = table.astype(ml_dtypes.bfloat16)
    low = (table - high.astype(np.float32)).astype(ml_dtypes.bfloat16)
    return high, low


def tables():
    index = np.arange(PATCH)
    phase = np.outer(index, index) % PATCH
    cosine = np.cos(2 * np.pi * phase / PATCH)
    sine = np.sin(2 * np.pi * phase / PATCH)
    down = np.zeros((PATCH + 16, PATCH))
    down[:HALF] = cosine[:HALF]
    down[HALF:PATCH] = sine[:HALF]
    down[PATCH:] = cosine[HALF]
    high, low = two_terms(down)
    down = np.concatenate([high, high, low], 1)
    high, low = two_terms(np.block([[cosine, -sine], [-sine, -cosine]]))
    across = np.concatenate([high, high, low], 0)
    high, low = two_terms(np.block([[cosine, sine], [-sine, cosine]]))
    back = np.concatenate([high, high, low], 0)
    share = np.full(HALF, 2.0)
    share[0] = 1.0
    up = np.concatenate([cosine[:, :HALF] * share, -sine[:, :HALF] * share], 1)
    up[:, HALF] = cosine[:, HALF]
    high, low = two_terms(up * (math.log2(math.e) / PATCH**3))
    up = np.concatenate([high, high, low], 1)
    return down, across, back, up


def passed_along(value, axis, steps):
    count = lax.axis_size(axis)
    initial, last = (max(0, -steps), min(count, count - steps))
    return lax.ppermute(value, axis, [(source, source + steps) for source in range(initial, last)])


def split(value):
    high = value.astype(bf16)
    return high, (value - high.astype(f32)).astype(bf16)


def dot(left, right):
    return lax.dot_general(left, right, (((1,), (0,)), ((), ())), preferred_element_type=f32)


def three(value, axis):
    high, low = split(value)
    return jnp.concatenate([high, low, high], axis)


def cross(spec, count):
    ar, ai = spec[:count, :PATCH], spec[:count, PATCH:]
    br, bi = spec[count:, :PATCH], spec[count:, PATCH:]
    return three(jnp.concatenate([ar * br + ai * bi, ar * bi - ai * br], 1), 1)


def flow_chunk(loads, base, down, across, back, up, u_high, u_low, u_edge, g_edge, stat):
    for s in range(2):
        for tile in range(0, TILES + 1, 2):
            n = min(2, TILES + 1 - tile)
            top, mid, halo = [split(cell) for cell in loads[s](tile, n)]
            for r, first in ((0, top), (1, halo)):
                right = jnp.concatenate([first[0], mid[0], first[1], mid[1], first[0], mid[0]], 0)
                u = dot(down[...], right)
                high, low = split(u[:PATCH])
                lanes = slice(tile * 128, (tile + n) * 128)
                u_high[s, r, :, lanes] = high
                u_low[s, r, :, lanes] = low
                u_edge[s, r, :, lanes] = u[PATCH : PATCH + 8]
    left_lanes = lax.broadcasted_iota(jnp.int32, (HALF, 128), 1) < HALF
    left_lanes8 = lax.broadcasted_iota(jnp.int32, (8, 128), 1) < HALF
    sub8 = lax.broadcasted_iota(jnp.int32, (8, 128), 0)
    count = TILES * 4
    blocks = []
    for s in range(2):
        for group in range(count // 8):
            rows = jnp.zeros((8, 128), f32)
            for k in range(8):
                p = group * 8 + k
                tile, parity, r = p // 4, (p // 2) % 2, p % 2
                window = u_edge[s, r, :, tile * 128 : (tile + 1) * 128]
                if parity:
                    window = jnp.where(left_lanes8, u_edge[s, r, :, (tile + 1) * 128 : (tile + 2) * 128], window)
                rows = jnp.where(sub8 == k, window, rows)
            blocks.append(rows)
    real_rows = jnp.concatenate([across[i * 256 : i * 256 + 128] for i in range(3)], 0)
    spec = dot(three(jnp.concatenate(blocks, 0), 1), real_rows)
    g_edge[...] = dot(cross(spec, count), back[...])[:, :128]

    def some(i, carry):
        left = []
        for s in range(2):
            for q in range(QUAD):
                lane = pl.multiple_of((i * QUAD + q) * 128, 128)
                for parity in range(2):
                    for r in range(2):
                        parts = []
                        for ref in (u_high, u_low):
                            for half in range(2):
                                rows = slice(half * HALF, (half + 1) * HALF)
                                window = ref[s, r, rows, pl.ds(lane, 128)]
                                if parity:
                                    window = jnp.where(left_lanes, ref[s, r, rows, pl.ds(lane + 128, 128)], window)
                                parts.append(window)
                        left.append(jnp.concatenate(parts + parts[:2], 1))
        spec = dot(jnp.concatenate(left, 0), across[...])
        g = dot(cross(spec, QUAD * 4 * HALF), back[...])
        for j in range(QUAD * 2):
            columns = []
            for r in range(2):
                p = j * 2 + r
                real = g[p * HALF : (p + 1) * HALF, :128]
                imag = g[p * HALF : (p + 1) * HALF, 128:]
                edge = g_edge[pl.ds(i * QUAD * 4 + p, 1), :]
                first = jnp.where(sub8 == 0, jnp.broadcast_to(edge, (8, 128)), imag[:8])
                columns.append(jnp.concatenate([real, first, imag[8:]], 0))
            scores = dot(up[...], three(jnp.concatenate(columns, 1), 0))
            for r in range(2):
                part = [scores[k * 8 : (k + 1) * 8, r * 128 : (r + 1) * 128] for k in range(16)]
                tops = part
                while len(tops) > 1:
                    tops = [jnp.maximum(tops[2 * z], tops[2 * z + 1]) for z in range(len(tops) // 2)]
                expo = [jnp.exp2(k - tops[0]) for k in part]
                plus, plus_rows = expo[7], expo[7]
                for k in range(6, 0, -1):
                    plus = plus + expo[k]
                    plus_rows = plus_rows + plus
                plus = plus + expo[0]
                minus, minus_rows = expo[8], expo[8]
                for k in range(9, 16):
                    minus = minus + expo[k]
                    minus_rows = minus_rows + minus
                at = base + r * HALF + i * QUAD * 2 + j
                stat[0, pl.ds(at, 1)] = tops[0][None]
                stat[1, pl.ds(at, 1)] = (plus + minus)[None]
                stat[2, pl.ds(at, 1)] = (plus_rows - minus_rows)[None]
        return carry

    lax.fori_loop(0, TILES // QUAD, some, 0)


def flow_rows(stat, at, half):
    top, total, rows = (stat[k, pl.ds(at, HALF)] for k in range(3))
    most = jnp.max(jnp.max(top, axis=1, keepdims=True), axis=2, keepdims=True)
    scale = jnp.exp2(top - most)
    sub = lax.broadcasted_iota(jnp.int32, (1, 8, 128), 1).astype(f32)
    total = total * scale
    rows = jnp.sum(rows * scale * 8.0 + total * sub, axis=1)
    total = jnp.sum(total, axis=1)
    lane = lax.broadcasted_iota(jnp.int32, (HALF, 128), 1)
    wrapped = jnp.where(lane >= HALF, lane - PATCH, lane).astype(f32)
    columns = jnp.sum(total * wrapped, axis=1, keepdims=True)
    rows = jnp.sum(rows, axis=1, keepdims=True)
    total = jnp.sum(total, axis=1, keepdims=True)
    here = lane == lax.broadcasted_iota(jnp.int32, (HALF, 128), 0) + half * HALF
    return [
        jnp.sum(jnp.where(here, jnp.broadcast_to(v / total, (HALF, 128)), 0.0), axis=0, keepdims=True)
        for v in (rows, columns)
    ]


def flow_kernel(a, b, down, across, back, up, out, u_high, u_low, u_edge, g_edge, stat):
    chunks = (SIDE - 1) // TILES

    def one(c, carry):
        half = c // chunks
        first = half * SIDE + (c % chunks) * TILES

        def loader(ref):
            def load(tile, n):
                lane = pl.multiple_of((first + tile) * 128, 128)
                return [ref[z * HALF : (z + 1) * HALF, pl.ds(lane, n * 128)] for z in range(3)]

            return load

        base = half * 128 + (c % chunks) * TILES * 2
        flow_chunk([loader(a), loader(b)], base, down, across, back, up, u_high, u_low, u_edge, g_edge, stat)
        return carry

    lax.fori_loop(0, 2 * chunks, one, 0)
    for half in range(2):
        for r in range(2):
            for k, row in enumerate(flow_rows(stat, half * 128 + r * HALF, half)):
                out[half, k, pl.ds(r, 1), :] = row


def flow_of(a, b):
    vmem = pl.BlockSpec(memory_space=pltpu.VMEM)
    wide = (TILES + 1) * 128
    return pl.pallas_call(
        flow_kernel,
        out_shape=jax.ShapeDtypeStruct((2, 2, 2, 128), f32),
        in_specs=[vmem] * 6,
        out_specs=vmem,
        scratch_shapes=[
            pltpu.VMEM((2, 2, 128, wide), bf16),
            pltpu.VMEM((2, 2, 128, wide), bf16),
            pltpu.VMEM((2, 2, 8, wide), f32),
            pltpu.VMEM((TILES * 4, 128), f32),
            pltpu.VMEM((3, 256, 8, 128), f32),
        ],
        compiler_params=pltpu.CompilerParams(vmem_limit_bytes=56 << 20),
    )(a, b, *(jnp.asarray(t) for t in tables()))


def entering(part, axis, combine, identity):
    place = lax.axis_index(axis)
    gathered = lax.all_gather(part, axis)
    state = jnp.zeros_like(part) + jnp.asarray(identity, part.dtype)

    def one(lap, state):
        return combine(state, lax.dynamic_index_in_dim(gathered, lap, 0, False))

    return lax.fori_loop(0, place, one, state)


def with_halo(block, sides, width):
    for axis, dim in sides:
        count = lax.axis_size(axis)
        forward = [(i, i + 1) for i in range(count - 1)]
        backward = [(target, source) for source, target in forward]
        low = lax.ppermute(
            lax.slice_in_dim(block, block.shape[dim] - width, None, axis=dim), axis, forward
        )
        high = lax.ppermute(lax.slice_in_dim(block, 0, width, axis=dim), axis, backward)
        block = jnp.concatenate([low, block, high], axis=dim)
    return block


def shards(sections, masks, carried):
    node_rows = sections.shape[1] // STRIDE
    node_cols = COLS // STRIDE
    below = passed_along(sections[:, :STRIDE], "tile", -1)
    extended = jnp.concatenate([sections, below], axis=1)[0]
    extended = jnp.pad(extended, ((0, 0), (0, 128)))
    left = extended[:, : SIDE * 128]
    right = extended[:, COLS // 2 :]
    a = jnp.concatenate([passed_along(left, "sec", 1), right], 1)
    b = jnp.concatenate([left, passed_along(right, "sec", -1)], 1)
    pieces = flow_of(a, b)
    flow = pieces[0] + passed_along(pieces[1], "sec", 1)
    later_sec = (lax.axis_index("sec") > 0).astype(jnp.float32)
    flow = jnp.where(lax.axis_index("sec") > 0, flow, carried)[None]
    pairs = masks.astype(jnp.float32) * later_sec
    before = entering(flow, "sec", lambda early, late: early + late, jnp.zeros_like(flow))
    start = before + flow
    upcoming = passed_along(jnp.concatenate([flow, pairs[:, None]], axis=1), "sec", -1)
    next_flow = upcoming[:, :2]
    next_pair = upcoming[:, 2]
    rows = lax.axis_index("tile") * node_rows + jnp.arange(node_rows)
    total_rows = node_rows * lax.axis_size("tile")
    cols = jnp.arange(node_cols)
    degree = (
        4.0
        - (rows == 0).astype(jnp.float32)[:, None]
        - (rows == total_rows - 1).astype(jnp.float32)[:, None]
        - (cols == 0).astype(jnp.float32)[None, :]
        - (cols == node_cols - 1).astype(jnp.float32)[None, :]
    )
    denom = (
        spring_weight * degree[None] + link_weight * pairs + link_weight * next_pair + anchor_weight
    )
    aligned = start
    for step in range(ITERS):
        grown = with_halo(aligned, (("sec", 0), ("tile", 2)), 1)
        middle = grown[1:2]
        centre = middle[:, :, 1:-1]
        sideways = jnp.pad(centre, ((0, 0), (0, 0), (0, 0), (1, 1)))
        beside = (
            middle[:, :, :-2] + middle[:, :, 2:] + sideways[:, :, :, :-2] + sideways[:, :, :, 2:]
        )
        before = grown[0:1, :, 1:-1]
        after = grown[2:3, :, 1:-1]
        total = (
            spring_weight * beside
            + link_weight * pairs[:, None] * (before + flow)
            + link_weight * next_pair[:, None] * (after - next_flow)
            + anchor_weight * start
        )
        aligned = total / denom[:, None]
    return (flow, aligned)


def solution(mesh):
    in_specs = (P("sec", "tile", None), P("sec", "tile", None), P(None, "tile", None))
    out_specs = (P("sec", None, "tile", None), P("sec", None, "tile", None))
    return jax.shard_map(shards, mesh=mesh, in_specs=in_specs, out_specs=out_specs, check_vma=False)
```

```python
import math

import jax
import jax.numpy as jnp
import ml_dtypes
import numpy as np
from jax import lax
from jax.experimental import pallas as pl
from jax.experimental.pallas import tpu as pltpu
from jax.sharding import PartitionSpec as P

COLS = 8192
PATCH = 128
STRIDE = 64
ITERS = 3
HALF = PATCH // 2
TILES = 8
QUAD = 4
SIDE = 33
CHUNKS = 4
MESH = pl.DeviceIdType.MESH

spring_weight = 1.0
link_weight = 4.0
anchor_weight = 0.5
bf16 = jnp.bfloat16
f32 = jnp.float32


def two_terms(table):
    table = table.astype(np.float32)
    high = table.astype(ml_dtypes.bfloat16)
    low = (table - high.astype(np.float32)).astype(ml_dtypes.bfloat16)
    return high, low


def tables():
    index = np.arange(PATCH)
    phase = np.outer(index, index) % PATCH
    cosine = np.cos(2 * np.pi * phase / PATCH)
    sine = np.sin(2 * np.pi * phase / PATCH)
    down = np.zeros((PATCH + 16, PATCH))
    down[:HALF] = cosine[:HALF]
    down[HALF:PATCH] = sine[:HALF]
    down[PATCH:] = cosine[HALF]
    high, low = two_terms(down)
    down = np.concatenate([high, high, low], 1)
    high, low = two_terms(np.block([[cosine, -sine], [-sine, -cosine]]))
    across = np.concatenate([high, high, low], 0)
    high, low = two_terms(np.block([[cosine, sine], [-sine, cosine]]))
    back = np.concatenate([high, high, low], 0)
    share = np.full(HALF, 2.0)
    share[0] = 1.0
    up = np.concatenate([cosine[:, :HALF] * share, -sine[:, :HALF] * share], 1)
    up[:, HALF] = cosine[:, HALF]
    high, low = two_terms(up * (math.log2(math.e) / PATCH**3))
    up = np.concatenate([high, high, low], 1)
    return down, across, back, up


def split(value):
    high = value.astype(bf16)
    return high, (value - high.astype(f32)).astype(bf16)


def dot(left, right):
    return lax.dot_general(left, right, (((1,), (0,)), ((), ())), preferred_element_type=f32)


def three(value, axis):
    high, low = split(value)
    return jnp.concatenate([high, low, high], axis)


def cross(spec, count):
    ar, ai = spec[:count, :PATCH], spec[:count, PATCH:]
    br, bi = spec[count:, :PATCH], spec[count:, PATCH:]
    return three(jnp.concatenate([ar * br + ai * bi, ar * bi - ai * br], 1), 1)


def flow_chunk(loads, base, down, across, back, up, u_high, u_low, u_edge, g_edge, stat):
    for s in range(2):
        for tile in range(0, TILES + 1, 2):
            n = min(2, TILES + 1 - tile)
            top, mid, halo = [split(cell) for cell in loads[s](tile, n)]
            for r, first in ((0, top), (1, halo)):
                right = jnp.concatenate([first[0], mid[0], first[1], mid[1], first[0], mid[0]], 0)
                u = dot(down[...], right)
                high, low = split(u[:PATCH])
                lanes = slice(tile * 128, (tile + n) * 128)
                u_high[s, r, :, lanes] = high
                u_low[s, r, :, lanes] = low
                u_edge[s, r, :, lanes] = u[PATCH : PATCH + 8]
    left_lanes = lax.broadcasted_iota(jnp.int32, (HALF, 128), 1) < HALF
    left_lanes8 = lax.broadcasted_iota(jnp.int32, (8, 128), 1) < HALF
    sub8 = lax.broadcasted_iota(jnp.int32, (8, 128), 0)
    count = TILES * 4
    blocks = []
    for s in range(2):
        for group in range(count // 8):
            rows = jnp.zeros((8, 128), f32)
            for k in range(8):
                p = group * 8 + k
                tile, parity, r = p // 4, (p // 2) % 2, p % 2
                window = u_edge[s, r, :, tile * 128 : (tile + 1) * 128]
                if parity:
                    window = jnp.where(left_lanes8, u_edge[s, r, :, (tile + 1) * 128 : (tile + 2) * 128], window)
                rows = jnp.where(sub8 == k, window, rows)
            blocks.append(rows)
    real_rows = jnp.concatenate([across[i * 256 : i * 256 + 128] for i in range(3)], 0)
    spec = dot(three(jnp.concatenate(blocks, 0), 1), real_rows)
    g_edge[...] = dot(cross(spec, count), back[...])[:, :128]

    def some(i, carry):
        left = []
        for s in range(2):
            for q in range(QUAD):
                lane = pl.multiple_of((i * QUAD + q) * 128, 128)
                for parity in range(2):
                    for r in range(2):
                        parts = []
                        for ref in (u_high, u_low):
                            for half in range(2):
                                rows = slice(half * HALF, (half + 1) * HALF)
                                window = ref[s, r, rows, pl.ds(lane, 128)]
                                if parity:
                                    window = jnp.where(left_lanes, ref[s, r, rows, pl.ds(lane + 128, 128)], window)
                                parts.append(window)
                        left.append(jnp.concatenate(parts + parts[:2], 1))
        spec = dot(jnp.concatenate(left, 0), across[...])
        g = dot(cross(spec, QUAD * 4 * HALF), back[...])
        for j in range(QUAD * 2):
            columns = []
            for r in range(2):
                p = j * 2 + r
                real = g[p * HALF : (p + 1) * HALF, :128]
                imag = g[p * HALF : (p + 1) * HALF, 128:]
                edge = g_edge[pl.ds(i * QUAD * 4 + p, 1), :]
                first = jnp.where(sub8 == 0, jnp.broadcast_to(edge, (8, 128)), imag[:8])
                columns.append(jnp.concatenate([real, first, imag[8:]], 0))
            scores = dot(up[...], three(jnp.concatenate(columns, 1), 0))
            for r in range(2):
                part = [scores[k * 8 : (k + 1) * 8, r * 128 : (r + 1) * 128] for k in range(16)]
                tops = part
                while len(tops) > 1:
                    tops = [jnp.maximum(tops[2 * z], tops[2 * z + 1]) for z in range(len(tops) // 2)]
                expo = [jnp.exp2(k - tops[0]) for k in part]
                plus, plus_rows = expo[7], expo[7]
                for k in range(6, 0, -1):
                    plus = plus + expo[k]
                    plus_rows = plus_rows + plus
                plus = plus + expo[0]
                minus, minus_rows = expo[8], expo[8]
                for k in range(9, 16):
                    minus = minus + expo[k]
                    minus_rows = minus_rows + minus
                at = base + r * HALF + i * QUAD * 2 + j
                stat[0, pl.ds(at, 1)] = tops[0][None]
                stat[1, pl.ds(at, 1)] = (plus + minus)[None]
                stat[2, pl.ds(at, 1)] = (plus_rows - minus_rows)[None]
        return carry

    lax.fori_loop(0, TILES // QUAD, some, 0)


def flow_rows(stat, at, half):
    top, total, rows = (stat[k, pl.ds(at, HALF)] for k in range(3))
    most = jnp.max(jnp.max(top, axis=1, keepdims=True), axis=2, keepdims=True)
    scale = jnp.exp2(top - most)
    sub = lax.broadcasted_iota(jnp.int32, (1, 8, 128), 1).astype(f32)
    total = total * scale
    rows = jnp.sum(rows * scale * 8.0 + total * sub, axis=1)
    total = jnp.sum(total, axis=1)
    lane = lax.broadcasted_iota(jnp.int32, (HALF, 128), 1)
    wrapped = jnp.where(lane >= HALF, lane - PATCH, lane).astype(f32)
    columns = jnp.sum(total * wrapped, axis=1, keepdims=True)
    rows = jnp.sum(rows, axis=1, keepdims=True)
    total = jnp.sum(total, axis=1, keepdims=True)
    here = lane == lax.broadcasted_iota(jnp.int32, (HALF, 128), 0) + half * HALF
    return [
        jnp.sum(jnp.where(here, jnp.broadcast_to(v / total, (HALF, 128)), 0.0), axis=0, keepdims=True)
        for v in (rows, columns)
    ]


def flow_kernel(x, down, across, back, up, out, strips, u_high, u_low, u_edge, g_edge, stat,
                own_sem, strip_send, strip_recv, halo_send, halo_recv, relay_send, relay_recv):
    sec, tile = lax.axis_index("sec"), lax.axis_index("tile")
    secs, tiles = lax.axis_size("sec"), lax.axis_size("tile")
    barrier = pltpu.get_barrier_semaphore()
    for place in (
        (lax.rem(sec + 1, secs), tile),
        (lax.rem(sec + secs - 1, secs), tile),
        (sec, lax.rem(tile + 1, tiles)),
        (sec, lax.rem(tile + tiles - 1, tiles)),
    ):
        pl.semaphore_signal(barrier, inc=1, device_id=place, device_id_type=MESH)
    width = TILES * 128

    def own(half):
        first, n = (0, SIDE) if half == 0 else (SIDE - 1, SIDE - 1)
        return pltpu.make_async_copy(
            x.at[:, pl.ds(first * 128, n * 128)],
            strips.at[1 - half, pl.ds(0, PATCH), pl.ds(half * SIDE * 128, n * 128)],
            own_sem.at[half],
        )

    for half in range(2):
        own(half).start()
    pl.semaphore_wait(barrier, 4)

    def spans(half, c, n):
        source = pl.multiple_of((half * (SIDE - 1) + c * TILES) * 128, 128)
        target = pl.multiple_of((half * SIDE + c * TILES) * 128, 128)
        return pl.ds(source, n), pl.ds(target, n)

    def strip(half, c, n=width):
        source, target = spans(half, c, n)
        return pltpu.make_async_remote_copy(
            x.at[:, source],
            strips.at[half, pl.ds(0, PATCH), target],
            strip_send.at[half, c],
            strip_recv.at[half, c],
            device_id=(lax.rem(sec + 1 - 2 * half + secs, secs), tile),
            device_id_type=MESH,
        )

    def halo(half, c, n=width):
        source, target = spans(half, c, n)
        return pltpu.make_async_remote_copy(
            x.at[pl.ds(0, HALF), source],
            strips.at[1 - half, pl.ds(PATCH, HALF), target],
            halo_send.at[half, c],
            halo_recv.at[half, c],
            device_id=(sec, lax.rem(tile + tiles - 1, tiles)),
            device_id_type=MESH,
        )

    def relay(half, c, n=width):
        _, target = spans(half, c, n)
        return pltpu.make_async_remote_copy(
            strips.at[half, pl.ds(0, HALF), target],
            strips.at[half, pl.ds(PATCH, HALF), target],
            relay_send.at[half, c],
            relay_recv.at[half, c],
            device_id=(sec, lax.rem(tile + tiles - 1, tiles)),
            device_id_type=MESH,
        )

    def gives(half):
        return jnp.logical_or(jnp.logical_and(half == 0, sec < secs - 1), jnp.logical_and(half == 1, sec > 0))

    def works(half):
        return jnp.logical_or(jnp.logical_and(half == 0, sec > 0), jnp.logical_and(half == 1, sec < secs - 1))

    above, under = tile > 0, tile < tiles - 1

    def both(p, q):
        return jnp.logical_and(p, q)

    def step(i):
        return lax.rem(i, 2), CHUNKS - 1 - i // 2

    @pl.when(gives(0))
    def _():
        strip(0, CHUNKS, 128).start()

    @pl.when(both(works(0), above))
    def _():
        halo(0, CHUNKS, 128).start()

    def begin(i, carry):
        half, c = step(i)

        @pl.when(gives(half))
        def _():
            strip(half, c).start()

        @pl.when(both(works(half), above))
        def _():
            halo(half, c).start()

        return carry

    lax.fori_loop(0, 2 * CHUNKS, begin, 0)
    for s in range(2):
        strips[s, :, (2 * SIDE - 1) * 128 :] = jnp.zeros((PATCH + HALF, 128), f32)

    @pl.when(jnp.logical_not(under))
    def _():
        for s in range(2):
            strips[s, PATCH:, : (2 * SIDE - 1) * 128] = jnp.zeros((HALF, (2 * SIDE - 1) * 128), f32)

    for half in range(2):
        own(half).wait()

    @pl.when(works(0))
    def _():
        strip(0, CHUNKS, 128).wait_recv()

        @pl.when(above)
        def _():
            relay(0, CHUNKS, 128).start()

    def arrive(half, c):
        @pl.when(works(half))
        def _():
            strip(half, c).wait_recv()

            @pl.when(above)
            def _():
                relay(half, c).start()

    arrive(*step(0))

    @pl.when(both(works(0), under))
    def _():
        halo(0, CHUNKS, 128).wait_recv()
        relay(0, CHUNKS, 128).wait_recv()

    def one(i, carry):
        half, c = step(i)

        @pl.when(i + 1 < 2 * CHUNKS)
        def _():
            arrive(*step(i + 1))

        @pl.when(works(half))
        def _():
            @pl.when(under)
            def _():
                halo(half, c).wait_recv()
                relay(half, c).wait_recv()

            def loader(s):
                def load(tile, n):
                    lane = pl.multiple_of((half * SIDE + c * TILES + tile) * 128, 128)
                    return [strips[s, z * HALF : (z + 1) * HALF, pl.ds(lane, n * 128)] for z in range(3)]

                return load

            base = half * PATCH + c * TILES * 2
            flow_chunk([loader(0), loader(1)], base, down, across, back, up, u_high, u_low, u_edge, g_edge, stat)

        return carry

    lax.fori_loop(0, 2 * CHUNKS, one, 0)
    for half in range(2):
        for r in range(2):
            for k, row in enumerate(flow_rows(stat, half * 128 + r * HALF, half)):
                out[half, k, pl.ds(r, 1), :] = row

    @pl.when(gives(0))
    def _():
        strip(0, CHUNKS, 128).wait_send()

    @pl.when(both(works(0), above))
    def _():
        halo(0, CHUNKS, 128).wait_send()
        relay(0, CHUNKS, 128).wait_send()

    def end(i, carry):
        half, c = step(i)

        @pl.when(gives(half))
        def _():
            strip(half, c).wait_send()

        @pl.when(both(works(half), above))
        def _():
            halo(half, c).wait_send()
            relay(half, c).wait_send()

        return carry

    lax.fori_loop(0, 2 * CHUNKS, end, 0)


def flow_of(x):
    vmem = pl.BlockSpec(memory_space=pltpu.VMEM)
    wide = (TILES + 1) * 128
    dma = pltpu.SemaphoreType.DMA
    return pl.pallas_call(
        flow_kernel,
        out_shape=jax.ShapeDtypeStruct((2, 2, 2, 128), f32),
        in_specs=[pl.BlockSpec(memory_space=pl.ANY)] + [vmem] * 4,
        out_specs=vmem,
        scratch_shapes=[
            pltpu.VMEM((2, PATCH + HALF, 2 * SIDE * 128), f32),
            pltpu.VMEM((2, 2, 128, wide), bf16),
            pltpu.VMEM((2, 2, 128, wide), bf16),
            pltpu.VMEM((2, 2, 8, wide), f32),
            pltpu.VMEM((TILES * 4, 128), f32),
            pltpu.VMEM((3, 256, 8, 128), f32),
            dma((2,)),
        ]
        + [dma((2, CHUNKS + 1))] * 6,
        compiler_params=pltpu.CompilerParams(vmem_limit_bytes=56 << 20, collective_id=0, has_side_effects=True),
    )(x, *(jnp.asarray(t) for t in tables()))


def relax_kernel(pieces, masks, carried, flow_out, aligned_out, blocks, result, sec_send, sec_recv, tile_send, tile_recv):
    sec, tile = lax.axis_index("sec"), lax.axis_index("tile")
    secs, tiles = lax.axis_size("sec"), lax.axis_size("tile")
    barrier = pltpu.get_barrier_semaphore()
    steps = (1, 2, tiles - 1, tiles - 2)
    slots = (1, 0, 3, 4)
    for k in range(1, secs):
        pl.semaphore_signal(barrier, inc=1, device_id=(lax.rem(sec + k, secs), tile), device_id_type=MESH)
    for k in steps:
        pl.semaphore_signal(barrier, inc=1, device_id=(sec, lax.rem(tile + k, tiles)), device_id_type=MESH)
    rows = [pieces[h, k] for h in range(2) for k in range(2)]
    rows += [masks[...].astype(f32), carried[0], carried[1], jnp.zeros((2, 128), f32)]
    blocks[2, pl.ds(sec, 1)] = jnp.concatenate(rows, 0)[None]
    pl.semaphore_wait(barrier, secs - 1 + len(steps))

    def to_sec(k, owner):
        return pltpu.make_async_remote_copy(
            blocks.at[2, owner],
            blocks.at[2, owner],
            sec_send.at[k],
            sec_recv.at[k],
            device_id=(lax.rem(sec + k, secs), tile),
            device_id_type=MESH,
        )

    for k in range(1, secs):
        to_sec(k, sec).start()
    for k in range(1, secs):
        to_sec(k, lax.rem(sec + secs - k, secs)).wait_recv()
    copies = [
        pltpu.make_async_remote_copy(
            blocks.at[2],
            blocks.at[slot],
            tile_send.at[n],
            tile_recv.at[n],
            device_id=(sec, lax.rem(tile + k, tiles)),
            device_id_type=MESH,
        )
        for n, (k, slot) in enumerate(zip(steps, slots))
    ]
    for copy in copies:
        copy.start()
    for copy in copies:
        copy.wait_recv()

    def window(get):
        return jnp.concatenate([get(0)[1:2], get(1), get(2), get(3), get(4)[0:1]], 0)

    flow = []
    for s in range(secs):
        if s == 0:
            flow.append([window(lambda d: blocks[d, 0, 10 + 2 * k : 12 + 2 * k]) for k in range(2)])
        else:
            flow.append([
                window(lambda d: blocks[d, s, 2 * k : 2 * k + 2] + blocks[d, s - 1, 4 + 2 * k : 6 + 2 * k])
                for k in range(2)
            ])
    zero = jnp.zeros((8, 128), f32)
    pairs = [zero] + [link_weight * window(lambda d: blocks[d, s, 8:10]) for s in range(1, secs)] + [zero]
    node = 2 * tile - 3 + lax.broadcasted_iota(jnp.int32, (8, 128), 0)
    column = lax.broadcasted_iota(jnp.int32, (8, 128), 1)
    last = 2 * tiles - 1
    inside = jnp.logical_and(node >= 0, node <= last)
    at_left, at_right = column == 0, column == 127

    def as_float(test):
        return jnp.where(test, 1.0, 0.0)

    degree = 4.0 - as_float(node == 0) - as_float(node == last) - as_float(at_left) - as_float(at_right)
    start = [[jnp.where(inside, v, 0.0) for v in flow[0]]]
    for s in range(1, secs):
        start.append([start[s - 1][k] + jnp.where(inside, flow[s][k], 0.0) for k in range(2)])
    inverse = [
        jnp.where(inside, 1.0 / (spring_weight * degree + pairs[s] + pairs[s + 1] + anchor_weight), 0.0)
        for s in range(secs)
    ]
    fixed = []
    for s in range(secs):
        row = []
        for k in range(2):
            v = anchor_weight * start[s][k]
            if s > 0:
                v = v + pairs[s] * flow[s][k]
            if s + 1 < secs:
                v = v - pairs[s + 1] * flow[s + 1][k]
            row.append(v)
        fixed.append(row)
    aligned = start
    for step in range(ITERS):
        new = []
        for s in range(secs):
            row = []
            for k in range(2):
                v = aligned[s][k]
                total = fixed[s][k] + spring_weight * (
                    pltpu.roll(v, 1, 0)
                    + pltpu.roll(v, 7, 0)
                    + jnp.where(at_left, 0.0, pltpu.roll(v, 1, 1))
                    + jnp.where(at_right, 0.0, pltpu.roll(v, 127, 1))
                )
                if s > 0:
                    total = total + pairs[s] * aligned[s - 1][k]
                if s + 1 < secs:
                    total = total + pairs[s + 1] * aligned[s + 1][k]
                row.append(jnp.where(inside, total * inverse[s], 0.0))
            new.append(row)
        aligned = new
    for s in range(secs):
        for k in range(2):
            result[s, k] = flow[s][k]
            result[s, 2 + k] = aligned[s][k]
    for k in range(2):
        flow_out[k] = result[sec, k][3:5]
        aligned_out[k] = result[sec, 2 + k][3:5]
    for k in range(1, secs):
        to_sec(k, sec).wait_send()
    for copy in copies:
        copy.wait_send()


def relaxed(pieces, masks, carried):
    vmem = pl.BlockSpec(memory_space=pltpu.VMEM)
    dma = pltpu.SemaphoreType.DMA
    secs = lax.axis_size("sec")
    shape = jax.ShapeDtypeStruct((2, 2, 128), f32)
    return pl.pallas_call(
        relax_kernel,
        out_shape=(shape, shape),
        in_specs=[vmem] * 3,
        out_specs=(vmem, vmem),
        scratch_shapes=[
            pltpu.VMEM((5, secs, 16, 128), f32),
            pltpu.VMEM((secs, 4, 8, 128), f32),
            dma((secs,)),
            dma((secs,)),
            dma((4,)),
            dma((4,)),
        ],
        compiler_params=pltpu.CompilerParams(collective_id=1, has_side_effects=True),
    )(pieces, masks, carried)


def shards(sections, masks, carried):
    flow, aligned = relaxed(flow_of(sections[0]), masks[0], carried)
    return flow[None], aligned[None]


def solution(mesh):
    in_specs = (P("sec", "tile", None), P("sec", "tile", None), P(None, "tile", None))
    out_specs = (P("sec", None, "tile", None), P("sec", None, "tile", None))
    return jax.shard_map(shards, mesh=mesh, in_specs=in_specs, out_specs=out_specs, check_vma=False)
```

```python
import math

import jax
import jax.numpy as jnp
import ml_dtypes
import numpy as np
from jax import lax
from jax.experimental import pallas as pl
from jax.experimental.pallas import tpu as pltpu
from jax.sharding import PartitionSpec as P

COLS = 8192
PATCH = 128
STRIDE = 64
ITERS = 3
HALF = PATCH // 2
TILES = 8
QUAD = 4
SIDE = 33
CHUNKS = 4
DETOUR = 3
MESH = pl.DeviceIdType.MESH

spring_weight = 1.0
link_weight = 4.0
anchor_weight = 0.5
bf16 = jnp.bfloat16
f32 = jnp.float32


def two_terms(table):
    table = table.astype(np.float32)
    high = table.astype(ml_dtypes.bfloat16)
    low = (table - high.astype(np.float32)).astype(ml_dtypes.bfloat16)
    return high, low


def tables():
    index = np.arange(PATCH)
    phase = np.outer(index, index) % PATCH
    cosine = np.cos(2 * np.pi * phase / PATCH)
    sine = np.sin(2 * np.pi * phase / PATCH)
    down = np.zeros((PATCH + 16, PATCH))
    down[:HALF] = cosine[:HALF]
    down[HALF:PATCH] = sine[:HALF]
    down[PATCH:] = cosine[HALF]
    high, low = two_terms(down)
    down = np.concatenate([high, high, low], 1)
    high, low = two_terms(np.block([[cosine, -sine], [-sine, -cosine]]))
    across = np.concatenate([high, high, low], 0)
    high, low = two_terms(np.block([[cosine, sine], [-sine, cosine]]))
    back = np.concatenate([high, high, low], 0)
    share = np.full(HALF, 2.0)
    share[0] = 1.0
    up = np.concatenate([cosine[:, :HALF] * share, -sine[:, :HALF] * share], 1)
    up[:, HALF] = cosine[:, HALF]
    high, low = two_terms(up * (math.log2(math.e) / PATCH**3))
    up = np.concatenate([high, high, low], 1)
    return down, across, back, up


def split(value):
    high = value.astype(bf16)
    return high, (value - high.astype(f32)).astype(bf16)


def dot(left, right):
    return lax.dot_general(left, right, (((1,), (0,)), ((), ())), preferred_element_type=f32)


def three(value, axis):
    high, low = split(value)
    return jnp.concatenate([high, low, high], axis)


def cross(spec, count):
    ar, ai = spec[:count, :PATCH], spec[:count, PATCH:]
    br, bi = spec[count:, :PATCH], spec[count:, PATCH:]
    return three(jnp.concatenate([ar * br + ai * bi, ar * bi - ai * br], 1), 1)


def flow_chunk(loads, base, down, across, back, up, u_high, u_low, u_edge, g_edge, stat):
    for s in range(2):
        for tile in range(0, TILES + 1, 2):
            n = min(2, TILES + 1 - tile)
            top, mid, halo = [split(cell) for cell in loads[s](tile, n)]
            for r, first in ((0, top), (1, halo)):
                right = jnp.concatenate([first[0], mid[0], first[1], mid[1], first[0], mid[0]], 0)
                u = dot(down[...], right)
                high, low = split(u[:PATCH])
                lanes = slice(tile * 128, (tile + n) * 128)
                u_high[s, r, :, lanes] = high
                u_low[s, r, :, lanes] = low
                u_edge[s, r, :, lanes] = u[PATCH : PATCH + 8]
    left_lanes = lax.broadcasted_iota(jnp.int32, (HALF, 128), 1) < HALF
    left_lanes8 = lax.broadcasted_iota(jnp.int32, (8, 128), 1) < HALF
    sub8 = lax.broadcasted_iota(jnp.int32, (8, 128), 0)
    count = TILES * 4
    blocks = []
    for s in range(2):
        for group in range(count // 8):
            rows = jnp.zeros((8, 128), f32)
            for k in range(8):
                p = group * 8 + k
                tile, parity, r = p // 4, (p // 2) % 2, p % 2
                window = u_edge[s, r, :, tile * 128 : (tile + 1) * 128]
                if parity:
                    window = jnp.where(left_lanes8, u_edge[s, r, :, (tile + 1) * 128 : (tile + 2) * 128], window)
                rows = jnp.where(sub8 == k, window, rows)
            blocks.append(rows)
    real_rows = jnp.concatenate([across[i * 256 : i * 256 + 128] for i in range(3)], 0)
    spec = dot(three(jnp.concatenate(blocks, 0), 1), real_rows)
    g_edge[...] = dot(cross(spec, count), back[...])[:, :128]

    def some(i, carry):
        left = []
        for s in range(2):
            for q in range(QUAD):
                lane = pl.multiple_of((i * QUAD + q) * 128, 128)
                for parity in range(2):
                    for r in range(2):
                        parts = []
                        for ref in (u_high, u_low):
                            for half in range(2):
                                rows = slice(half * HALF, (half + 1) * HALF)
                                window = ref[s, r, rows, pl.ds(lane, 128)]
                                if parity:
                                    window = jnp.where(left_lanes, ref[s, r, rows, pl.ds(lane + 128, 128)], window)
                                parts.append(window)
                        left.append(jnp.concatenate(parts + parts[:2], 1))
        spec = dot(jnp.concatenate(left, 0), across[...])
        g = dot(cross(spec, QUAD * 4 * HALF), back[...])
        for j in range(QUAD * 2):
            columns = []
            for r in range(2):
                p = j * 2 + r
                real = g[p * HALF : (p + 1) * HALF, :128]
                imag = g[p * HALF : (p + 1) * HALF, 128:]
                edge = g_edge[pl.ds(i * QUAD * 4 + p, 1), :]
                first = jnp.where(sub8 == 0, jnp.broadcast_to(edge, (8, 128)), imag[:8])
                columns.append(jnp.concatenate([real, first, imag[8:]], 0))
            scores = dot(up[...], three(jnp.concatenate(columns, 1), 0))
            for r in range(2):
                part = [scores[k * 8 : (k + 1) * 8, r * 128 : (r + 1) * 128] for k in range(16)]
                tops = part
                while len(tops) > 1:
                    tops = [jnp.maximum(tops[2 * z], tops[2 * z + 1]) for z in range(len(tops) // 2)]
                expo = [jnp.exp2(k - tops[0]) for k in part]
                plus, plus_rows = expo[7], expo[7]
                for k in range(6, 0, -1):
                    plus = plus + expo[k]
                    plus_rows = plus_rows + plus
                plus = plus + expo[0]
                minus, minus_rows = expo[8], expo[8]
                for k in range(9, 16):
                    minus = minus + expo[k]
                    minus_rows = minus_rows + minus
                at = base + r * HALF + i * QUAD * 2 + j
                stat[0, pl.ds(at, 1)] = tops[0][None]
                stat[1, pl.ds(at, 1)] = (plus + minus)[None]
                stat[2, pl.ds(at, 1)] = (plus_rows - minus_rows)[None]
        return carry

    lax.fori_loop(0, TILES // QUAD, some, 0)


def flow_rows(stat, at, half):
    top, total, rows = (stat[k, pl.ds(at, HALF)] for k in range(3))
    most = jnp.max(jnp.max(top, axis=1, keepdims=True), axis=2, keepdims=True)
    scale = jnp.exp2(top - most)
    sub = lax.broadcasted_iota(jnp.int32, (1, 8, 128), 1).astype(f32)
    total = total * scale
    rows = jnp.sum(rows * scale * 8.0 + total * sub, axis=1)
    total = jnp.sum(total, axis=1)
    lane = lax.broadcasted_iota(jnp.int32, (HALF, 128), 1)
    wrapped = jnp.where(lane >= HALF, lane - PATCH, lane).astype(f32)
    columns = jnp.sum(total * wrapped, axis=1, keepdims=True)
    rows = jnp.sum(rows, axis=1, keepdims=True)
    total = jnp.sum(total, axis=1, keepdims=True)
    here = lane == lax.broadcasted_iota(jnp.int32, (HALF, 128), 0) + half * HALF
    return [
        jnp.sum(jnp.where(here, jnp.broadcast_to(v / total, (HALF, 128)), 0.0), axis=0, keepdims=True)
        for v in (rows, columns)
    ]


def flow_kernel(x, down, across, back, up, out, strips, u_high, u_low, u_edge, g_edge, stat,
                own_sem, strip_send, strip_recv, halo_send, halo_recv, relay_send, relay_recv):
    sec, tile = lax.axis_index("sec"), lax.axis_index("tile")
    secs, tiles = lax.axis_size("sec"), lax.axis_size("tile")
    barrier = pltpu.get_barrier_semaphore()
    for place in (
        (lax.rem(sec + 1, secs), tile),
        (lax.rem(sec + secs - 1, secs), tile),
        (sec, lax.rem(tile + 1, tiles)),
        (sec, lax.rem(tile + tiles - 1, tiles)),
    ):
        pl.semaphore_signal(barrier, inc=1, device_id=place, device_id_type=MESH)
    swapped = tile + 2 - 4 * lax.rem(tile // 2, 2)
    first, last = sec == 0, sec == secs - 1
    middle = secs // 2
    lower, upper = sec == middle - 1, sec == middle

    @pl.when(jnp.logical_or(first, last))
    def _():
        for there in (middle - 1, middle):
            pl.semaphore_signal(barrier, inc=1, device_id=(there, swapped), device_id_type=MESH)

    @pl.when(jnp.logical_or(lower, upper))
    def _():
        for there in (0, secs - 1):
            pl.semaphore_signal(barrier, inc=1, device_id=(there, swapped), device_id_type=MESH)

    width = TILES * 128

    def own(half):
        first, n = (0, SIDE) if half == 0 else (SIDE - 1, SIDE - 1)
        return pltpu.make_async_copy(
            x.at[:, pl.ds(first * 128, n * 128)],
            strips.at[1 - half, pl.ds(0, PATCH), pl.ds(half * SIDE * 128, n * 128)],
            own_sem.at[half],
        )

    for half in range(2):
        own(half).start()
    outer = jnp.logical_or(jnp.logical_or(first, last), jnp.logical_or(lower, upper))
    pl.semaphore_wait(barrier, jnp.where(outer, 6, 4))

    def spans(half, c, n):
        source = pl.multiple_of((half * (SIDE - 1) + c * TILES) * 128, 128)
        target = pl.multiple_of((half * SIDE + c * TILES) * 128, 128)
        return pl.ds(source, n), pl.ds(target, n)

    def strip(half, c, n=width):
        source, target = spans(half, c, n)
        return pltpu.make_async_remote_copy(
            x.at[:, source],
            strips.at[half, pl.ds(0, PATCH), target],
            strip_send.at[half, c],
            strip_recv.at[half, c],
            device_id=(lax.rem(sec + 1 - 2 * half + secs, secs), tile),
            device_id_type=MESH,
        )

    def detour(half, c):
        source, _ = spans(half, c, width)
        _, target = spans(1 - half, c, width)
        return pltpu.make_async_remote_copy(
            x.at[:, source],
            strips.at[1 - half, pl.ds(0, PATCH), target],
            strip_send.at[half, c],
            strip_recv.at[1 - half, c],
            device_id=((secs - 1) * (1 - half), swapped),
            device_id_type=MESH,
        )

    def onward(half, c):
        _, source = spans(half, c, width)
        _, target = spans(1 - half, c, width)
        return pltpu.make_async_remote_copy(
            strips.at[half, pl.ds(0, PATCH), source],
            strips.at[1 - half, pl.ds(0, PATCH), target],
            strip_send.at[1 - half, c],
            strip_recv.at[1 - half, c],
            device_id=(middle - 1 + half, swapped),
            device_id_type=MESH,
        )

    def around(half, c):
        mine = jnp.logical_or(jnp.logical_and(half == 0, lower), jnp.logical_and(half == 1, upper))
        return jnp.logical_and(mine, c < DETOUR)

    def passes(half, c):
        mine = jnp.logical_or(jnp.logical_and(half == 0, first), jnp.logical_and(half == 1, last))
        return jnp.logical_and(mine, c < DETOUR)

    def halo(half, c, n=width):
        source, target = spans(half, c, n)
        return pltpu.make_async_remote_copy(
            x.at[pl.ds(0, HALF), source],
            strips.at[1 - half, pl.ds(PATCH, HALF), target],
            halo_send.at[half, c],
            halo_recv.at[half, c],
            device_id=(sec, lax.rem(tile + tiles - 1, tiles)),
            device_id_type=MESH,
        )

    def relay(half, c, n=width):
        _, target = spans(half, c, n)
        return pltpu.make_async_remote_copy(
            strips.at[half, pl.ds(0, HALF), target],
            strips.at[half, pl.ds(PATCH, HALF), target],
            relay_send.at[half, c],
            relay_recv.at[half, c],
            device_id=(sec, lax.rem(tile + tiles - 1, tiles)),
            device_id_type=MESH,
        )

    def gives(half):
        return jnp.logical_or(jnp.logical_and(half == 0, sec < secs - 1), jnp.logical_and(half == 1, sec > 0))

    def works(half):
        return jnp.logical_or(jnp.logical_and(half == 0, sec > 0), jnp.logical_and(half == 1, sec < secs - 1))

    above, under = tile > 0, tile < tiles - 1

    def both(p, q):
        return jnp.logical_and(p, q)

    def step(i):
        return lax.rem(i, 2), CHUNKS - 1 - i // 2

    @pl.when(gives(0))
    def _():
        strip(0, CHUNKS, 128).start()

    @pl.when(both(works(0), above))
    def _():
        halo(0, CHUNKS, 128).start()

    def begin(i, carry):
        half, c = step(i)

        @pl.when(both(gives(half), jnp.logical_not(around(half, c))))
        def _():
            strip(half, c).start()

        @pl.when(around(half, c))
        def _():
            detour(half, c).start()

        @pl.when(both(works(half), above))
        def _():
            halo(half, c).start()

        return carry

    lax.fori_loop(0, 2 * CHUNKS, begin, 0)
    for s in range(2):
        strips[s, :, (2 * SIDE - 1) * 128 :] = jnp.zeros((PATCH + HALF, 128), f32)

    @pl.when(jnp.logical_not(under))
    def _():
        for s in range(2):
            strips[s, PATCH:, : (2 * SIDE - 1) * 128] = jnp.zeros((HALF, (2 * SIDE - 1) * 128), f32)

    for half in range(2):
        own(half).wait()

    @pl.when(works(0))
    def _():
        strip(0, CHUNKS, 128).wait_recv()

        @pl.when(above)
        def _():
            relay(0, CHUNKS, 128).start()

    def arrive(half, c):
        @pl.when(works(half))
        def _():
            strip(half, c).wait_recv()

            @pl.when(above)
            def _():
                relay(half, c).start()

        @pl.when(passes(half, c))
        def _():
            detour(1 - half, c).wait_recv()
            onward(half, c).start()

    arrive(*step(0))

    @pl.when(both(works(0), under))
    def _():
        halo(0, CHUNKS, 128).wait_recv()
        relay(0, CHUNKS, 128).wait_recv()

    def one(i, carry):
        half, c = step(i)

        @pl.when(i + 1 < 2 * CHUNKS)
        def _():
            arrive(*step(i + 1))

        @pl.when(works(half))
        def _():
            @pl.when(under)
            def _():
                halo(half, c).wait_recv()
                relay(half, c).wait_recv()

            def loader(s):
                def load(tile, n):
                    lane = pl.multiple_of((half * SIDE + c * TILES + tile) * 128, 128)
                    return [strips[s, z * HALF : (z + 1) * HALF, pl.ds(lane, n * 128)] for z in range(3)]

                return load

            base = half * PATCH + c * TILES * 2
            flow_chunk([loader(0), loader(1)], base, down, across, back, up, u_high, u_low, u_edge, g_edge, stat)

        return carry

    lax.fori_loop(0, 2 * CHUNKS, one, 0)
    for half in range(2):
        for r in range(2):
            for k, row in enumerate(flow_rows(stat, half * 128 + r * HALF, half)):
                out[half, k, pl.ds(r, 1), :] = row

    @pl.when(gives(0))
    def _():
        strip(0, CHUNKS, 128).wait_send()

    @pl.when(both(works(0), above))
    def _():
        halo(0, CHUNKS, 128).wait_send()
        relay(0, CHUNKS, 128).wait_send()

    def end(i, carry):
        half, c = step(i)

        @pl.when(both(gives(half), jnp.logical_not(around(half, c))))
        def _():
            strip(half, c).wait_send()

        @pl.when(around(half, c))
        def _():
            detour(half, c).wait_send()

        @pl.when(passes(half, c))
        def _():
            onward(half, c).wait_send()

        @pl.when(both(works(half), above))
        def _():
            halo(half, c).wait_send()
            relay(half, c).wait_send()

        return carry

    lax.fori_loop(0, 2 * CHUNKS, end, 0)


def flow_of(x):
    vmem = pl.BlockSpec(memory_space=pltpu.VMEM)
    wide = (TILES + 1) * 128
    dma = pltpu.SemaphoreType.DMA
    return pl.pallas_call(
        flow_kernel,
        out_shape=jax.ShapeDtypeStruct((2, 2, 2, 128), f32),
        in_specs=[pl.BlockSpec(memory_space=pl.ANY)] + [vmem] * 4,
        out_specs=vmem,
        scratch_shapes=[
            pltpu.VMEM((2, PATCH + HALF, 2 * SIDE * 128), f32),
            pltpu.VMEM((2, 2, 128, wide), bf16),
            pltpu.VMEM((2, 2, 128, wide), bf16),
            pltpu.VMEM((2, 2, 8, wide), f32),
            pltpu.VMEM((TILES * 4, 128), f32),
            pltpu.VMEM((3, 256, 8, 128), f32),
            dma((2,)),
        ]
        + [dma((2, CHUNKS + 1))] * 6,
        compiler_params=pltpu.CompilerParams(vmem_limit_bytes=56 << 20, collective_id=0, has_side_effects=True),
    )(x, *(jnp.asarray(t) for t in tables()))


def relax_kernel(pieces, masks, carried, flow_out, aligned_out, blocks, result, sec_send, sec_recv, tile_send, tile_recv):
    sec, tile = lax.axis_index("sec"), lax.axis_index("tile")
    secs, tiles = lax.axis_size("sec"), lax.axis_size("tile")
    barrier = pltpu.get_barrier_semaphore()
    steps = (1, 2, tiles - 1, tiles - 2)
    slots = (1, 0, 3, 4)
    for k in range(1, secs):
        pl.semaphore_signal(barrier, inc=1, device_id=(lax.rem(sec + k, secs), tile), device_id_type=MESH)
    for k in steps:
        pl.semaphore_signal(barrier, inc=1, device_id=(sec, lax.rem(tile + k, tiles)), device_id_type=MESH)
    rows = [pieces[h, k] for h in range(2) for k in range(2)]
    rows += [masks[...].astype(f32), carried[0], carried[1], jnp.zeros((2, 128), f32)]
    blocks[2, pl.ds(sec, 1)] = jnp.concatenate(rows, 0)[None]
    pl.semaphore_wait(barrier, secs - 1 + len(steps))

    def to_sec(k, owner):
        return pltpu.make_async_remote_copy(
            blocks.at[2, owner],
            blocks.at[2, owner],
            sec_send.at[k],
            sec_recv.at[k],
            device_id=(lax.rem(sec + k, secs), tile),
            device_id_type=MESH,
        )

    for k in range(1, secs):
        to_sec(k, sec).start()
    for k in range(1, secs):
        to_sec(k, lax.rem(sec + secs - k, secs)).wait_recv()
    copies = [
        pltpu.make_async_remote_copy(
            blocks.at[2],
            blocks.at[slot],
            tile_send.at[n],
            tile_recv.at[n],
            device_id=(sec, lax.rem(tile + k, tiles)),
            device_id_type=MESH,
        )
        for n, (k, slot) in enumerate(zip(steps, slots))
    ]
    for copy in copies:
        copy.start()
    for copy in copies:
        copy.wait_recv()

    def window(get):
        return jnp.concatenate([get(0)[1:2], get(1), get(2), get(3), get(4)[0:1]], 0)

    flow = []
    for s in range(secs):
        if s == 0:
            flow.append([window(lambda d: blocks[d, 0, 10 + 2 * k : 12 + 2 * k]) for k in range(2)])
        else:
            flow.append([
                window(lambda d: blocks[d, s, 2 * k : 2 * k + 2] + blocks[d, s - 1, 4 + 2 * k : 6 + 2 * k])
                for k in range(2)
            ])
    zero = jnp.zeros((8, 128), f32)
    pairs = [zero] + [link_weight * window(lambda d: blocks[d, s, 8:10]) for s in range(1, secs)] + [zero]
    node = 2 * tile - 3 + lax.broadcasted_iota(jnp.int32, (8, 128), 0)
    column = lax.broadcasted_iota(jnp.int32, (8, 128), 1)
    last = 2 * tiles - 1
    inside = jnp.logical_and(node >= 0, node <= last)
    at_left, at_right = column == 0, column == 127

    def as_float(test):
        return jnp.where(test, 1.0, 0.0)

    degree = 4.0 - as_float(node == 0) - as_float(node == last) - as_float(at_left) - as_float(at_right)
    start = [[jnp.where(inside, v, 0.0) for v in flow[0]]]
    for s in range(1, secs):
        start.append([start[s - 1][k] + jnp.where(inside, flow[s][k], 0.0) for k in range(2)])
    inverse = [
        jnp.where(inside, 1.0 / (spring_weight * degree + pairs[s] + pairs[s + 1] + anchor_weight), 0.0)
        for s in range(secs)
    ]
    fixed = []
    for s in range(secs):
        row = []
        for k in range(2):
            v = anchor_weight * start[s][k]
            if s > 0:
                v = v + pairs[s] * flow[s][k]
            if s + 1 < secs:
                v = v - pairs[s + 1] * flow[s + 1][k]
            row.append(v)
        fixed.append(row)
    aligned = start
    for step in range(ITERS):
        new = []
        for s in range(secs):
            row = []
            for k in range(2):
                v = aligned[s][k]
                total = fixed[s][k] + spring_weight * (
                    pltpu.roll(v, 1, 0)
                    + pltpu.roll(v, 7, 0)
                    + jnp.where(at_left, 0.0, pltpu.roll(v, 1, 1))
                    + jnp.where(at_right, 0.0, pltpu.roll(v, 127, 1))
                )
                if s > 0:
                    total = total + pairs[s] * aligned[s - 1][k]
                if s + 1 < secs:
                    total = total + pairs[s + 1] * aligned[s + 1][k]
                row.append(jnp.where(inside, total * inverse[s], 0.0))
            new.append(row)
        aligned = new
    for s in range(secs):
        for k in range(2):
            result[s, k] = flow[s][k]
            result[s, 2 + k] = aligned[s][k]
    for k in range(2):
        flow_out[k] = result[sec, k][3:5]
        aligned_out[k] = result[sec, 2 + k][3:5]
    for k in range(1, secs):
        to_sec(k, sec).wait_send()
    for copy in copies:
        copy.wait_send()


def relaxed(pieces, masks, carried):
    vmem = pl.BlockSpec(memory_space=pltpu.VMEM)
    dma = pltpu.SemaphoreType.DMA
    secs = lax.axis_size("sec")
    shape = jax.ShapeDtypeStruct((2, 2, 128), f32)
    return pl.pallas_call(
        relax_kernel,
        out_shape=(shape, shape),
        in_specs=[vmem] * 3,
        out_specs=(vmem, vmem),
        scratch_shapes=[
            pltpu.VMEM((5, secs, 16, 128), f32),
            pltpu.VMEM((secs, 4, 8, 128), f32),
            dma((secs,)),
            dma((secs,)),
            dma((4,)),
            dma((4,)),
        ],
        compiler_params=pltpu.CompilerParams(collective_id=1, has_side_effects=True),
    )(pieces, masks, carried)


def shards(sections, masks, carried):
    flow, aligned = relaxed(flow_of(sections[0]), masks[0], carried)
    return flow[None], aligned[None]


def solution(mesh):
    in_specs = (P("sec", "tile", None), P("sec", "tile", None), P(None, "tile", None))
    out_specs = (P("sec", None, "tile", None), P("sec", None, "tile", None))
    return jax.shard_map(shards, mesh=mesh, in_specs=in_specs, out_specs=out_specs, check_vma=False)
```

```python
import math

import jax
import jax.numpy as jnp
import ml_dtypes
import numpy as np
from jax import lax
from jax.experimental import pallas as pl
from jax.experimental.pallas import tpu as pltpu
from jax.sharding import PartitionSpec as P

COLS = 8192
PATCH = 128
STRIDE = 64
ITERS = 3
HALF = PATCH // 2
TILES = 8
QUAD = 8
SIDE = 33
CHUNKS = 4
DETOUR = 3
MESH = pl.DeviceIdType.MESH

spring_weight = 1.0
link_weight = 4.0
anchor_weight = 0.5
bf16 = jnp.bfloat16
f32 = jnp.float32


def two_terms(table):
    table = table.astype(np.float32)
    high = table.astype(ml_dtypes.bfloat16)
    low = (table - high.astype(np.float32)).astype(ml_dtypes.bfloat16)
    return high, low


def tables():
    index = np.arange(PATCH)
    phase = np.outer(index, index) % PATCH
    cosine = np.cos(2 * np.pi * phase / PATCH)
    sine = np.sin(2 * np.pi * phase / PATCH)
    down = np.zeros((PATCH + 16, PATCH))
    down[:HALF] = cosine[:HALF]
    down[HALF:PATCH] = sine[:HALF]
    down[PATCH:] = cosine[HALF]
    high, low = two_terms(down)
    down = np.concatenate([high, high, low], 1)
    high, low = two_terms(np.block([[cosine, -sine], [-sine, -cosine]]))
    across = np.concatenate([high, high, low], 0)
    high, low = two_terms(np.block([[cosine, sine], [-sine, cosine]]))
    back = np.concatenate([high, high, low], 0)
    share = np.full(HALF, 2.0)
    share[0] = 1.0
    up = np.concatenate([cosine[:, :HALF] * share, -sine[:, :HALF] * share], 1)
    up[:, HALF] = cosine[:, HALF]
    high, low = two_terms(up * (math.log2(math.e) / PATCH**3))
    up = np.concatenate([high, high, low], 1)
    return down, across, back, up


def split(value):
    high = value.astype(bf16)
    return high, (value - high.astype(f32)).astype(bf16)


def dot(left, right):
    return lax.dot_general(left, right, (((1,), (0,)), ((), ())), preferred_element_type=f32)


def three(value, axis):
    high, low = split(value)
    return jnp.concatenate([high, low, high], axis)


def cross(spec, count):
    ar, ai = spec[:count, :PATCH], spec[:count, PATCH:]
    br, bi = spec[count:, :PATCH], spec[count:, PATCH:]
    return three(jnp.concatenate([ar * br + ai * bi, ar * bi - ai * br], 1), 1)


def flow_chunk(loads, base, down, across, back, up, u_high, u_low, u_edge, g_edge, stat):
    for s in range(2):
        for tile in range(0, TILES + 1, 2):
            n = min(2, TILES + 1 - tile)
            top, mid, halo = [split(cell) for cell in loads[s](tile, n)]
            for r, first in ((0, top), (1, halo)):
                right = jnp.concatenate([first[0], mid[0], first[1], mid[1], first[0], mid[0]], 0)
                u = dot(down[...], right)
                high, low = split(u[:PATCH])
                lanes = slice(tile * 128, (tile + n) * 128)
                u_high[s, r, :, lanes] = high
                u_low[s, r, :, lanes] = low
                u_edge[s, r, :, lanes] = u[PATCH : PATCH + 8]
    left_lanes = lax.broadcasted_iota(jnp.int32, (HALF, 128), 1) < HALF
    left_lanes8 = lax.broadcasted_iota(jnp.int32, (8, 128), 1) < HALF
    sub8 = lax.broadcasted_iota(jnp.int32, (8, 128), 0)
    count = TILES * 4
    blocks = []
    for s in range(2):
        for group in range(count // 8):
            rows = jnp.zeros((8, 128), f32)
            for k in range(8):
                p = group * 8 + k
                tile, parity, r = p // 4, (p // 2) % 2, p % 2
                window = u_edge[s, r, :, tile * 128 : (tile + 1) * 128]
                if parity:
                    window = jnp.where(left_lanes8, u_edge[s, r, :, (tile + 1) * 128 : (tile + 2) * 128], window)
                rows = jnp.where(sub8 == k, window, rows)
            blocks.append(rows)
    real_rows = jnp.concatenate([across[i * 256 : i * 256 + 128] for i in range(3)], 0)
    spec = dot(three(jnp.concatenate(blocks, 0), 1), real_rows)
    g_edge[...] = dot(cross(spec, count), back[...])[:, :128]

    def some(i, carry):
        left = []
        for s in range(2):
            for q in range(QUAD):
                lane = pl.multiple_of((i * QUAD + q) * 128, 128)
                for parity in range(2):
                    for r in range(2):
                        parts = []
                        for ref in (u_high, u_low):
                            for half in range(2):
                                rows = slice(half * HALF, (half + 1) * HALF)
                                window = ref[s, r, rows, pl.ds(lane, 128)]
                                if parity:
                                    window = jnp.where(left_lanes, ref[s, r, rows, pl.ds(lane + 128, 128)], window)
                                parts.append(window)
                        left.append(jnp.concatenate(parts + parts[:2], 1))
        spec = dot(jnp.concatenate(left, 0), across[...])
        g = dot(cross(spec, QUAD * 4 * HALF), back[...])
        for j in range(QUAD * 2):
            columns = []
            for r in range(2):
                p = j * 2 + r
                real = g[p * HALF : (p + 1) * HALF, :128]
                imag = g[p * HALF : (p + 1) * HALF, 128:]
                edge = g_edge[pl.ds(i * QUAD * 4 + p, 1), :]
                first = jnp.where(sub8 == 0, jnp.broadcast_to(edge, (8, 128)), imag[:8])
                columns.append(jnp.concatenate([real, first, imag[8:]], 0))
            scores = dot(up[...], three(jnp.concatenate(columns, 1), 0))
            for r in range(2):
                part = [scores[k * 8 : (k + 1) * 8, r * 128 : (r + 1) * 128] for k in range(16)]
                tops = part
                while len(tops) > 1:
                    tops = [jnp.maximum(tops[2 * z], tops[2 * z + 1]) for z in range(len(tops) // 2)]
                expo = [jnp.exp2(k - tops[0]) for k in part]
                plus, plus_rows = expo[7], expo[7]
                for k in range(6, 0, -1):
                    plus = plus + expo[k]
                    plus_rows = plus_rows + plus
                plus = plus + expo[0]
                minus, minus_rows = expo[8], expo[8]
                for k in range(9, 16):
                    minus = minus + expo[k]
                    minus_rows = minus_rows + minus
                at = base + r * HALF + i * QUAD * 2 + j
                stat[0, pl.ds(at, 1)] = tops[0][None]
                stat[1, pl.ds(at, 1)] = (plus + minus)[None]
                stat[2, pl.ds(at, 1)] = (plus_rows - minus_rows)[None]
        return carry

    lax.fori_loop(0, TILES // QUAD, some, 0)


def flow_rows(stat, at, half):
    top, total, rows = (stat[k, pl.ds(at, HALF)] for k in range(3))
    most = jnp.max(jnp.max(top, axis=1, keepdims=True), axis=2, keepdims=True)
    scale = jnp.exp2(top - most)
    sub = lax.broadcasted_iota(jnp.int32, (1, 8, 128), 1).astype(f32)
    total = total * scale
    rows = jnp.sum(rows * scale * 8.0 + total * sub, axis=1)
    total = jnp.sum(total, axis=1)
    lane = lax.broadcasted_iota(jnp.int32, (HALF, 128), 1)
    wrapped = jnp.where(lane >= HALF, lane - PATCH, lane).astype(f32)
    columns = jnp.sum(total * wrapped, axis=1, keepdims=True)
    rows = jnp.sum(rows, axis=1, keepdims=True)
    total = jnp.sum(total, axis=1, keepdims=True)
    here = lane == lax.broadcasted_iota(jnp.int32, (HALF, 128), 0) + half * HALF
    return [
        jnp.sum(jnp.where(here, jnp.broadcast_to(v / total, (HALF, 128)), 0.0), axis=0, keepdims=True)
        for v in (rows, columns)
    ]


def flow_kernel(x, down, across, back, up, out, strips, u_high, u_low, u_edge, g_edge, stat,
                own_sem, strip_send, strip_recv, halo_send, halo_recv, relay_send, relay_recv):
    sec, tile = lax.axis_index("sec"), lax.axis_index("tile")
    secs, tiles = lax.axis_size("sec"), lax.axis_size("tile")
    barrier = pltpu.get_barrier_semaphore()
    for place in (
        (lax.rem(sec + 1, secs), tile),
        (lax.rem(sec + secs - 1, secs), tile),
        (sec, lax.rem(tile + 1, tiles)),
        (sec, lax.rem(tile + tiles - 1, tiles)),
    ):
        pl.semaphore_signal(barrier, inc=1, device_id=place, device_id_type=MESH)
    swapped = tile + 2 - 4 * lax.rem(tile // 2, 2)
    first, last = sec == 0, sec == secs - 1
    middle = secs // 2
    lower, upper = sec == middle - 1, sec == middle

    @pl.when(jnp.logical_or(first, last))
    def _():
        for there in (middle - 1, middle):
            pl.semaphore_signal(barrier, inc=1, device_id=(there, swapped), device_id_type=MESH)

    @pl.when(jnp.logical_or(lower, upper))
    def _():
        for there in (0, secs - 1):
            pl.semaphore_signal(barrier, inc=1, device_id=(there, swapped), device_id_type=MESH)

    width = TILES * 128

    def own(half):
        first, n = (0, SIDE) if half == 0 else (SIDE - 1, SIDE - 1)
        return pltpu.make_async_copy(
            x.at[:, pl.ds(first * 128, n * 128)],
            strips.at[1 - half, pl.ds(0, PATCH), pl.ds(half * SIDE * 128, n * 128)],
            own_sem.at[half],
        )

    for half in range(2):
        own(half).start()
    outer = jnp.logical_or(jnp.logical_or(first, last), jnp.logical_or(lower, upper))
    pl.semaphore_wait(barrier, jnp.where(outer, 6, 4))

    def spans(half, c, n):
        source = pl.multiple_of((half * (SIDE - 1) + c * TILES) * 128, 128)
        target = pl.multiple_of((half * SIDE + c * TILES) * 128, 128)
        return pl.ds(source, n), pl.ds(target, n)

    def strip(half, c, n=width):
        source, target = spans(half, c, n)
        return pltpu.make_async_remote_copy(
            x.at[:, source],
            strips.at[half, pl.ds(0, PATCH), target],
            strip_send.at[half, c],
            strip_recv.at[half, c],
            device_id=(lax.rem(sec + 1 - 2 * half + secs, secs), tile),
            device_id_type=MESH,
        )

    def detour(half, c):
        source, _ = spans(half, c, width)
        _, target = spans(1 - half, c, width)
        return pltpu.make_async_remote_copy(
            x.at[:, source],
            strips.at[1 - half, pl.ds(0, PATCH), target],
            strip_send.at[half, c],
            strip_recv.at[1 - half, c],
            device_id=((secs - 1) * (1 - half), swapped),
            device_id_type=MESH,
        )

    def onward(half, c):
        _, source = spans(half, c, width)
        _, target = spans(1 - half, c, width)
        return pltpu.make_async_remote_copy(
            strips.at[half, pl.ds(0, PATCH), source],
            strips.at[1 - half, pl.ds(0, PATCH), target],
            strip_send.at[1 - half, c],
            strip_recv.at[1 - half, c],
            device_id=(middle - 1 + half, swapped),
            device_id_type=MESH,
        )

    def around(half, c):
        mine = jnp.logical_or(jnp.logical_and(half == 0, lower), jnp.logical_and(half == 1, upper))
        return jnp.logical_and(mine, c < DETOUR)

    def passes(half, c):
        mine = jnp.logical_or(jnp.logical_and(half == 0, first), jnp.logical_and(half == 1, last))
        return jnp.logical_and(mine, c < DETOUR)

    def halo(half, c, n=width):
        source, target = spans(half, c, n)
        return pltpu.make_async_remote_copy(
            x.at[pl.ds(0, HALF), source],
            strips.at[1 - half, pl.ds(PATCH, HALF), target],
            halo_send.at[half, c],
            halo_recv.at[half, c],
            device_id=(sec, lax.rem(tile + tiles - 1, tiles)),
            device_id_type=MESH,
        )

    def relay(half, c, n=width):
        _, target = spans(half, c, n)
        return pltpu.make_async_remote_copy(
            strips.at[half, pl.ds(0, HALF), target],
            strips.at[half, pl.ds(PATCH, HALF), target],
            relay_send.at[half, c],
            relay_recv.at[half, c],
            device_id=(sec, lax.rem(tile + tiles - 1, tiles)),
            device_id_type=MESH,
        )

    def gives(half):
        return jnp.logical_or(jnp.logical_and(half == 0, sec < secs - 1), jnp.logical_and(half == 1, sec > 0))

    def works(half):
        return jnp.logical_or(jnp.logical_and(half == 0, sec > 0), jnp.logical_and(half == 1, sec < secs - 1))

    above, under = tile > 0, tile < tiles - 1

    def both(p, q):
        return jnp.logical_and(p, q)

    def step(i):
        apart = jnp.logical_or(lower, upper)
        half = jnp.where(apart, lax.rem(i // CHUNKS + jnp.where(upper, 1, 0), 2), lax.rem(i, 2))
        return half, CHUNKS - 1 - jnp.where(apart, lax.rem(i, CHUNKS), i // 2)

    @pl.when(gives(0))
    def _():
        strip(0, CHUNKS, 128).start()

    @pl.when(both(works(0), above))
    def _():
        halo(0, CHUNKS, 128).start()

    def begin(i, carry):
        half, c = step(i)

        @pl.when(both(gives(half), jnp.logical_not(around(half, c))))
        def _():
            strip(half, c).start()

        @pl.when(around(half, c))
        def _():
            detour(half, c).start()

        @pl.when(both(works(half), above))
        def _():
            halo(half, c).start()

        return carry

    lax.fori_loop(0, 2 * CHUNKS, begin, 0)
    for s in range(2):
        strips[s, :, (2 * SIDE - 1) * 128 :] = jnp.zeros((PATCH + HALF, 128), f32)

    @pl.when(jnp.logical_not(under))
    def _():
        for s in range(2):
            strips[s, PATCH:, : (2 * SIDE - 1) * 128] = jnp.zeros((HALF, (2 * SIDE - 1) * 128), f32)

    for half in range(2):
        own(half).wait()

    @pl.when(works(0))
    def _():
        strip(0, CHUNKS, 128).wait_recv()

        @pl.when(above)
        def _():
            relay(0, CHUNKS, 128).start()

    def arrive(half, c):
        @pl.when(works(half))
        def _():
            strip(half, c).wait_recv()

            @pl.when(above)
            def _():
                relay(half, c).start()

        @pl.when(passes(half, c))
        def _():
            detour(1 - half, c).wait_recv()
            onward(half, c).start()

    arrive(*step(0))

    @pl.when(both(works(0), under))
    def _():
        halo(0, CHUNKS, 128).wait_recv()
        relay(0, CHUNKS, 128).wait_recv()

    def one(i, carry):
        half, c = step(i)

        @pl.when(i + 1 < 2 * CHUNKS)
        def _():
            arrive(*step(i + 1))

        @pl.when(works(half))
        def _():
            @pl.when(under)
            def _():
                halo(half, c).wait_recv()
                relay(half, c).wait_recv()

            def loader(s):
                def load(tile, n):
                    lane = pl.multiple_of((half * SIDE + c * TILES + tile) * 128, 128)
                    return [strips[s, z * HALF : (z + 1) * HALF, pl.ds(lane, n * 128)] for z in range(3)]

                return load

            base = half * PATCH + c * TILES * 2
            flow_chunk([loader(0), loader(1)], base, down, across, back, up, u_high, u_low, u_edge, g_edge, stat)

        return carry

    lax.fori_loop(0, 2 * CHUNKS, one, 0)
    for half in range(2):
        for r in range(2):
            for k, row in enumerate(flow_rows(stat, half * 128 + r * HALF, half)):
                out[half, k, pl.ds(r, 1), :] = row

    @pl.when(gives(0))
    def _():
        strip(0, CHUNKS, 128).wait_send()

    @pl.when(both(works(0), above))
    def _():
        halo(0, CHUNKS, 128).wait_send()
        relay(0, CHUNKS, 128).wait_send()

    def end(i, carry):
        half, c = step(i)

        @pl.when(both(gives(half), jnp.logical_not(around(half, c))))
        def _():
            strip(half, c).wait_send()

        @pl.when(around(half, c))
        def _():
            detour(half, c).wait_send()

        @pl.when(passes(half, c))
        def _():
            onward(half, c).wait_send()

        @pl.when(both(works(half), above))
        def _():
            halo(half, c).wait_send()
            relay(half, c).wait_send()

        return carry

    lax.fori_loop(0, 2 * CHUNKS, end, 0)


def flow_of(x):
    vmem = pl.BlockSpec(memory_space=pltpu.VMEM)
    wide = (TILES + 1) * 128
    dma = pltpu.SemaphoreType.DMA
    return pl.pallas_call(
        flow_kernel,
        out_shape=jax.ShapeDtypeStruct((2, 2, 2, 128), f32),
        in_specs=[pl.BlockSpec(memory_space=pl.ANY)] + [vmem] * 4,
        out_specs=vmem,
        scratch_shapes=[
            pltpu.VMEM((2, PATCH + HALF, 2 * SIDE * 128), f32),
            pltpu.VMEM((2, 2, 128, wide), bf16),
            pltpu.VMEM((2, 2, 128, wide), bf16),
            pltpu.VMEM((2, 2, 8, wide), f32),
            pltpu.VMEM((TILES * 4, 128), f32),
            pltpu.VMEM((3, 256, 8, 128), f32),
            dma((2,)),
        ]
        + [dma((2, CHUNKS + 1))] * 6,
        compiler_params=pltpu.CompilerParams(vmem_limit_bytes=56 << 20, collective_id=0, has_side_effects=True),
    )(x, *(jnp.asarray(t) for t in tables()))


def relax_kernel(pieces, masks, carried, flow_out, aligned_out, blocks, result, sec_send, sec_recv, tile_send, tile_recv):
    sec, tile = lax.axis_index("sec"), lax.axis_index("tile")
    secs, tiles = lax.axis_size("sec"), lax.axis_size("tile")
    barrier = pltpu.get_barrier_semaphore()
    steps = (1, 2, tiles - 1, tiles - 2)
    slots = (1, 0, 3, 4)
    for k in range(1, secs):
        pl.semaphore_signal(barrier, inc=1, device_id=(lax.rem(sec + k, secs), tile), device_id_type=MESH)
    for k in steps:
        pl.semaphore_signal(barrier, inc=1, device_id=(sec, lax.rem(tile + k, tiles)), device_id_type=MESH)
    rows = [pieces[h, k] for h in range(2) for k in range(2)]
    rows += [masks[...].astype(f32), carried[0], carried[1], jnp.zeros((2, 128), f32)]
    blocks[2, pl.ds(sec, 1)] = jnp.concatenate(rows, 0)[None]
    pl.semaphore_wait(barrier, secs - 1 + len(steps))

    def to_sec(k, owner):
        return pltpu.make_async_remote_copy(
            blocks.at[2, owner],
            blocks.at[2, owner],
            sec_send.at[k],
            sec_recv.at[k],
            device_id=(lax.rem(sec + k, secs), tile),
            device_id_type=MESH,
        )

    for k in range(1, secs):
        to_sec(k, sec).start()
    for k in range(1, secs):
        to_sec(k, lax.rem(sec + secs - k, secs)).wait_recv()
    copies = [
        pltpu.make_async_remote_copy(
            blocks.at[2],
            blocks.at[slot],
            tile_send.at[n],
            tile_recv.at[n],
            device_id=(sec, lax.rem(tile + k, tiles)),
            device_id_type=MESH,
        )
        for n, (k, slot) in enumerate(zip(steps, slots))
    ]
    for copy in copies:
        copy.start()
    for copy in copies:
        copy.wait_recv()

    def window(get):
        return jnp.concatenate([get(0)[1:2], get(1), get(2), get(3), get(4)[0:1]], 0)

    flow = []
    for s in range(secs):
        if s == 0:
            flow.append([window(lambda d: blocks[d, 0, 10 + 2 * k : 12 + 2 * k]) for k in range(2)])
        else:
            flow.append([
                window(lambda d: blocks[d, s, 2 * k : 2 * k + 2] + blocks[d, s - 1, 4 + 2 * k : 6 + 2 * k])
                for k in range(2)
            ])
    zero = jnp.zeros((8, 128), f32)
    pairs = [zero] + [link_weight * window(lambda d: blocks[d, s, 8:10]) for s in range(1, secs)] + [zero]
    node = 2 * tile - 3 + lax.broadcasted_iota(jnp.int32, (8, 128), 0)
    column = lax.broadcasted_iota(jnp.int32, (8, 128), 1)
    last = 2 * tiles - 1
    inside = jnp.logical_and(node >= 0, node <= last)
    at_left, at_right = column == 0, column == 127

    def as_float(test):
        return jnp.where(test, 1.0, 0.0)

    degree = 4.0 - as_float(node == 0) - as_float(node == last) - as_float(at_left) - as_float(at_right)
    start = [[jnp.where(inside, v, 0.0) for v in flow[0]]]
    for s in range(1, secs):
        start.append([start[s - 1][k] + jnp.where(inside, flow[s][k], 0.0) for k in range(2)])
    inverse = [
        jnp.where(inside, 1.0 / (spring_weight * degree + pairs[s] + pairs[s + 1] + anchor_weight), 0.0)
        for s in range(secs)
    ]
    fixed = []
    for s in range(secs):
        row = []
        for k in range(2):
            v = anchor_weight * start[s][k]
            if s > 0:
                v = v + pairs[s] * flow[s][k]
            if s + 1 < secs:
                v = v - pairs[s + 1] * flow[s + 1][k]
            row.append(v)
        fixed.append(row)
    aligned = start
    for step in range(ITERS):
        new = []
        for s in range(secs):
            row = []
            for k in range(2):
                v = aligned[s][k]
                total = fixed[s][k] + spring_weight * (
                    pltpu.roll(v, 1, 0)
                    + pltpu.roll(v, 7, 0)
                    + jnp.where(at_left, 0.0, pltpu.roll(v, 1, 1))
                    + jnp.where(at_right, 0.0, pltpu.roll(v, 127, 1))
                )
                if s > 0:
                    total = total + pairs[s] * aligned[s - 1][k]
                if s + 1 < secs:
                    total = total + pairs[s + 1] * aligned[s + 1][k]
                row.append(jnp.where(inside, total * inverse[s], 0.0))
            new.append(row)
        aligned = new
    for s in range(secs):
        for k in range(2):
            result[s, k] = flow[s][k]
            result[s, 2 + k] = aligned[s][k]
    for k in range(2):
        flow_out[k] = result[sec, k][3:5]
        aligned_out[k] = result[sec, 2 + k][3:5]
    for k in range(1, secs):
        to_sec(k, sec).wait_send()
    for copy in copies:
        copy.wait_send()


def relaxed(pieces, masks, carried):
    vmem = pl.BlockSpec(memory_space=pltpu.VMEM)
    dma = pltpu.SemaphoreType.DMA
    secs = lax.axis_size("sec")
    shape = jax.ShapeDtypeStruct((2, 2, 128), f32)
    return pl.pallas_call(
        relax_kernel,
        out_shape=(shape, shape),
        in_specs=[vmem] * 3,
        out_specs=(vmem, vmem),
        scratch_shapes=[
            pltpu.VMEM((5, secs, 16, 128), f32),
            pltpu.VMEM((secs, 4, 8, 128), f32),
            dma((secs,)),
            dma((secs,)),
            dma((4,)),
            dma((4,)),
        ],
        compiler_params=pltpu.CompilerParams(collective_id=1, has_side_effects=True),
    )(pieces, masks, carried)


def shards(sections, masks, carried):
    flow, aligned = relaxed(flow_of(sections[0]), masks[0], carried)
    return flow[None], aligned[None]


def solution(mesh):
    in_specs = (P("sec", "tile", None), P("sec", "tile", None), P(None, "tile", None))
    out_specs = (P("sec", None, "tile", None), P("sec", None, "tile", None))
    return jax.shard_map(shards, mesh=mesh, in_specs=in_specs, out_specs=out_specs, check_vma=False)
```

```python
import math

import jax
import jax.numpy as jnp
import ml_dtypes
import numpy as np
from jax import lax
from jax.experimental import pallas as pl
from jax.experimental.pallas import tpu as pltpu
from jax.sharding import PartitionSpec as P

COLS = 8192
PATCH = 128
STRIDE = 64
ITERS = 3
HALF = PATCH // 2
TILES = 8
QUAD = 8
SIDE = 33
CHUNKS = 4
DETOUR = 3
MESH = pl.DeviceIdType.MESH

spring_weight = 1.0
link_weight = 4.0
anchor_weight = 0.5
bf16 = jnp.bfloat16
f32 = jnp.float32


def two_terms(table):
    table = table.astype(np.float32)
    high = table.astype(ml_dtypes.bfloat16)
    low = (table - high.astype(np.float32)).astype(ml_dtypes.bfloat16)
    return high, low


def tables():
    index = np.arange(PATCH)
    phase = np.outer(index, index) % PATCH
    cosine = np.cos(2 * np.pi * phase / PATCH)
    sine = np.sin(2 * np.pi * phase / PATCH)
    down = np.zeros((PATCH + 16, PATCH))
    down[:HALF] = cosine[:HALF]
    down[HALF:PATCH] = sine[:HALF]
    down[PATCH:] = cosine[HALF]
    high, low = two_terms(down)
    down = np.concatenate([high, high, low], 1)
    high, low = two_terms(np.block([[cosine, -sine], [-sine, -cosine]]))
    across = np.concatenate([high, high, low], 0)
    high, low = two_terms(np.block([[cosine, sine], [-sine, cosine]]))
    back = np.concatenate([high, high, low], 0)
    share = np.full(HALF, 2.0)
    share[0] = 1.0
    up = np.concatenate([cosine[:, :HALF] * share, -sine[:, :HALF] * share], 1)
    up[:, HALF] = cosine[:, HALF]
    high, low = two_terms(up * (math.log2(math.e) / PATCH**3))
    up = np.concatenate([high, high, low], 1)
    return down, across, back, up


def split(value):
    high = value.astype(bf16)
    return high, (value - high.astype(f32)).astype(bf16)


def dot(left, right):
    return lax.dot_general(left, right, (((1,), (0,)), ((), ())), preferred_element_type=f32)


def three(value, axis):
    high, low = split(value)
    return jnp.concatenate([high, low, high], axis)


def cross(spec, count):
    ar, ai = spec[:count, :PATCH], spec[:count, PATCH:]
    br, bi = spec[count:, :PATCH], spec[count:, PATCH:]
    return three(jnp.concatenate([ar * br + ai * bi, ar * bi - ai * br], 1), 1)


def flow_chunk(loads, base, down, across, back, up, u_high, u_low, u_edge, g_edge, stat, between):
    for s in range(2):
        for tile in range(0, TILES + 1, 2):
            n = min(2, TILES + 1 - tile)
            top, mid, halo = [split(cell) for cell in loads[s](tile, n)]
            for r, first in ((0, top), (1, halo)):
                right = jnp.concatenate([first[0], mid[0], first[1], mid[1], first[0], mid[0]], 0)
                u = dot(down[...], right)
                high, low = split(u[:PATCH])
                lanes = slice(tile * 128, (tile + n) * 128)
                u_high[s, r, :, lanes] = high
                u_low[s, r, :, lanes] = low
                u_edge[s, r, :, lanes] = u[PATCH : PATCH + 8]
    left_lanes = lax.broadcasted_iota(jnp.int32, (HALF, 128), 1) < HALF
    left_lanes8 = lax.broadcasted_iota(jnp.int32, (8, 128), 1) < HALF
    sub8 = lax.broadcasted_iota(jnp.int32, (8, 128), 0)
    count = TILES * 4
    blocks = []
    for s in range(2):
        for group in range(count // 8):
            rows = jnp.zeros((8, 128), f32)
            for k in range(8):
                p = group * 8 + k
                tile, parity, r = p // 4, (p // 2) % 2, p % 2
                window = u_edge[s, r, :, tile * 128 : (tile + 1) * 128]
                if parity:
                    window = jnp.where(left_lanes8, u_edge[s, r, :, (tile + 1) * 128 : (tile + 2) * 128], window)
                rows = jnp.where(sub8 == k, window, rows)
            blocks.append(rows)
    real_rows = jnp.concatenate([across[i * 256 : i * 256 + 128] for i in range(3)], 0)
    spec = dot(three(jnp.concatenate(blocks, 0), 1), real_rows)
    g_edge[...] = dot(cross(spec, count), back[...])[:, :128]
    between()

    def some(i, carry):
        left = []
        for s in range(2):
            for q in range(QUAD):
                lane = pl.multiple_of((i * QUAD + q) * 128, 128)
                for parity in range(2):
                    for r in range(2):
                        parts = []
                        for ref in (u_high, u_low):
                            for half in range(2):
                                rows = slice(half * HALF, (half + 1) * HALF)
                                window = ref[s, r, rows, pl.ds(lane, 128)]
                                if parity:
                                    window = jnp.where(left_lanes, ref[s, r, rows, pl.ds(lane + 128, 128)], window)
                                parts.append(window)
                        left.append(jnp.concatenate(parts + parts[:2], 1))
        spec = dot(jnp.concatenate(left, 0), across[...])
        g = dot(cross(spec, QUAD * 4 * HALF), back[...])
        for j in range(QUAD * 2):
            columns = []
            for r in range(2):
                p = j * 2 + r
                real = g[p * HALF : (p + 1) * HALF, :128]
                imag = g[p * HALF : (p + 1) * HALF, 128:]
                edge = g_edge[pl.ds(i * QUAD * 4 + p, 1), :]
                first = jnp.where(sub8 == 0, jnp.broadcast_to(edge, (8, 128)), imag[:8])
                columns.append(jnp.concatenate([real, first, imag[8:]], 0))
            scores = dot(up[...], three(jnp.concatenate(columns, 1), 0))
            for r in range(2):
                part = [scores[k * 8 : (k + 1) * 8, r * 128 : (r + 1) * 128] for k in range(16)]
                tops = part
                while len(tops) > 1:
                    tops = [jnp.maximum(tops[2 * z], tops[2 * z + 1]) for z in range(len(tops) // 2)]
                expo = [jnp.exp2(k - tops[0]) for k in part]
                plus, plus_rows = expo[7], expo[7]
                for k in range(6, 0, -1):
                    plus = plus + expo[k]
                    plus_rows = plus_rows + plus
                plus = plus + expo[0]
                minus, minus_rows = expo[8], expo[8]
                for k in range(9, 16):
                    minus = minus + expo[k]
                    minus_rows = minus_rows + minus
                at = base + r * HALF + i * QUAD * 2 + j
                stat[0, pl.ds(at, 1)] = tops[0][None]
                stat[1, pl.ds(at, 1)] = (plus + minus)[None]
                stat[2, pl.ds(at, 1)] = (plus_rows - minus_rows)[None]
        return carry

    lax.fori_loop(0, TILES // QUAD, some, 0)


def flow_rows(stat, at, half):
    top, total, rows = (stat[k, pl.ds(at, HALF)] for k in range(3))
    most = jnp.max(jnp.max(top, axis=1, keepdims=True), axis=2, keepdims=True)
    scale = jnp.exp2(top - most)
    sub = lax.broadcasted_iota(jnp.int32, (1, 8, 128), 1).astype(f32)
    total = total * scale
    rows = jnp.sum(rows * scale * 8.0 + total * sub, axis=1)
    total = jnp.sum(total, axis=1)
    lane = lax.broadcasted_iota(jnp.int32, (HALF, 128), 1)
    wrapped = jnp.where(lane >= HALF, lane - PATCH, lane).astype(f32)
    columns = jnp.sum(total * wrapped, axis=1, keepdims=True)
    rows = jnp.sum(rows, axis=1, keepdims=True)
    total = jnp.sum(total, axis=1, keepdims=True)
    here = lane == lax.broadcasted_iota(jnp.int32, (HALF, 128), 0) + half * HALF
    return [
        jnp.sum(jnp.where(here, jnp.broadcast_to(v / total, (HALF, 128)), 0.0), axis=0, keepdims=True)
        for v in (rows, columns)
    ]


def flow_kernel(x, down, across, back, up, out, strips, u_high, u_low, u_edge, g_edge, stat,
                own_sem, strip_send, strip_recv, halo_send, halo_recv, relay_send, relay_recv):
    sec, tile = lax.axis_index("sec"), lax.axis_index("tile")
    secs, tiles = lax.axis_size("sec"), lax.axis_size("tile")
    barrier = pltpu.get_barrier_semaphore()
    for place in (
        (lax.rem(sec + 1, secs), tile),
        (lax.rem(sec + secs - 1, secs), tile),
        (sec, lax.rem(tile + 1, tiles)),
        (sec, lax.rem(tile + tiles - 1, tiles)),
    ):
        pl.semaphore_signal(barrier, inc=1, device_id=place, device_id_type=MESH)
    swapped = tile + 2 - 4 * lax.rem(tile // 2, 2)
    first, last = sec == 0, sec == secs - 1
    middle = secs // 2
    lower, upper = sec == middle - 1, sec == middle

    @pl.when(jnp.logical_or(first, last))
    def _():
        for there in (middle - 1, middle):
            pl.semaphore_signal(barrier, inc=1, device_id=(there, swapped), device_id_type=MESH)

    @pl.when(jnp.logical_or(lower, upper))
    def _():
        for there in (0, secs - 1):
            pl.semaphore_signal(barrier, inc=1, device_id=(there, swapped), device_id_type=MESH)

    width = TILES * 128

    def own(half):
        first, n = (0, SIDE) if half == 0 else (SIDE - 1, SIDE - 1)
        return pltpu.make_async_copy(
            x.at[:, pl.ds(first * 128, n * 128)],
            strips.at[1 - half, pl.ds(0, PATCH), pl.ds(half * SIDE * 128, n * 128)],
            own_sem.at[half],
        )

    for half in range(2):
        own(half).start()
    outer = jnp.logical_or(jnp.logical_or(first, last), jnp.logical_or(lower, upper))
    pl.semaphore_wait(barrier, jnp.where(outer, 6, 4))

    def spans(half, c, n):
        source = pl.multiple_of((half * (SIDE - 1) + c * TILES) * 128, 128)
        target = pl.multiple_of((half * SIDE + c * TILES) * 128, 128)
        return pl.ds(source, n), pl.ds(target, n)

    def strip(half, c, n=width):
        source, target = spans(half, c, n)
        return pltpu.make_async_remote_copy(
            x.at[:, source],
            strips.at[half, pl.ds(0, PATCH), target],
            strip_send.at[half, c],
            strip_recv.at[half, c],
            device_id=(lax.rem(sec + 1 - 2 * half + secs, secs), tile),
            device_id_type=MESH,
        )

    def detour(half, c):
        source, _ = spans(half, c, width)
        _, target = spans(1 - half, c, width)
        return pltpu.make_async_remote_copy(
            x.at[:, source],
            strips.at[1 - half, pl.ds(0, PATCH), target],
            strip_send.at[half, c],
            strip_recv.at[1 - half, c],
            device_id=((secs - 1) * (1 - half), swapped),
            device_id_type=MESH,
        )

    def onward(half, c):
        _, source = spans(half, c, width)
        _, target = spans(1 - half, c, width)
        return pltpu.make_async_remote_copy(
            strips.at[half, pl.ds(0, PATCH), source],
            strips.at[1 - half, pl.ds(0, PATCH), target],
            strip_send.at[1 - half, c],
            strip_recv.at[1 - half, c],
            device_id=(middle - 1 + half, swapped),
            device_id_type=MESH,
        )

    def around(half, c):
        mine = jnp.logical_or(jnp.logical_and(half == 0, lower), jnp.logical_and(half == 1, upper))
        return jnp.logical_and(mine, c < DETOUR)

    def passes(half, c):
        mine = jnp.logical_or(jnp.logical_and(half == 0, first), jnp.logical_and(half == 1, last))
        return jnp.logical_and(mine, c < DETOUR)

    def halo(half, c, n=width):
        source, target = spans(half, c, n)
        return pltpu.make_async_remote_copy(
            x.at[pl.ds(0, HALF), source],
            strips.at[1 - half, pl.ds(PATCH, HALF), target],
            halo_send.at[half, c],
            halo_recv.at[half, c],
            device_id=(sec, lax.rem(tile + tiles - 1, tiles)),
            device_id_type=MESH,
        )

    def relay(half, c, n=width):
        _, target = spans(half, c, n)
        return pltpu.make_async_remote_copy(
            strips.at[half, pl.ds(0, HALF), target],
            strips.at[half, pl.ds(PATCH, HALF), target],
            relay_send.at[half, c],
            relay_recv.at[half, c],
            device_id=(sec, lax.rem(tile + tiles - 1, tiles)),
            device_id_type=MESH,
        )

    def gives(half):
        return jnp.logical_or(jnp.logical_and(half == 0, sec < secs - 1), jnp.logical_and(half == 1, sec > 0))

    def works(half):
        return jnp.logical_or(jnp.logical_and(half == 0, sec > 0), jnp.logical_and(half == 1, sec < secs - 1))

    above, under = tile > 0, tile < tiles - 1

    def both(p, q):
        return jnp.logical_and(p, q)

    def step(i):
        apart = jnp.logical_or(lower, upper)
        half = jnp.where(apart, lax.rem(i // CHUNKS + jnp.where(upper, 1, 0), 2), lax.rem(i, 2))
        return half, CHUNKS - 1 - jnp.where(apart, lax.rem(i, CHUNKS), i // 2)

    @pl.when(gives(0))
    def _():
        strip(0, CHUNKS, 128).start()

    @pl.when(both(works(0), above))
    def _():
        halo(0, CHUNKS, 128).start()

    def begin(i, carry):
        half, c = step(i)

        @pl.when(both(gives(half), jnp.logical_not(around(half, c))))
        def _():
            strip(half, c).start()

        @pl.when(around(half, c))
        def _():
            detour(half, c).start()

        @pl.when(both(works(half), above))
        def _():
            halo(half, c).start()

        return carry

    lax.fori_loop(0, 2 * CHUNKS, begin, 0)
    for s in range(2):
        strips[s, :, (2 * SIDE - 1) * 128 :] = jnp.zeros((PATCH + HALF, 128), f32)

    @pl.when(jnp.logical_not(under))
    def _():
        for s in range(2):
            strips[s, PATCH:, : (2 * SIDE - 1) * 128] = jnp.zeros((HALF, (2 * SIDE - 1) * 128), f32)

    for half in range(2):
        own(half).wait()

    @pl.when(works(0))
    def _():
        strip(0, CHUNKS, 128).wait_recv()

        @pl.when(above)
        def _():
            relay(0, CHUNKS, 128).start()

    def arrive(half, c):
        @pl.when(works(half))
        def _():
            strip(half, c).wait_recv()

            @pl.when(above)
            def _():
                relay(half, c).start()

        @pl.when(passes(half, c))
        def _():
            detour(1 - half, c).wait_recv()
            onward(half, c).start()

    arrive(*step(0))

    @pl.when(both(works(0), under))
    def _():
        halo(0, CHUNKS, 128).wait_recv()
        relay(0, CHUNKS, 128).wait_recv()

    def one(i, carry):
        half, c = step(i)

        def advance():
            @pl.when(i + 1 < 2 * CHUNKS)
            def _():
                arrive(*step(i + 1))

        pl.when(jnp.logical_not(works(half)))(advance)

        @pl.when(works(half))
        def _():
            @pl.when(under)
            def _():
                halo(half, c).wait_recv()
                relay(half, c).wait_recv()

            def loader(s):
                def load(tile, n):
                    lane = pl.multiple_of((half * SIDE + c * TILES + tile) * 128, 128)
                    return [strips[s, z * HALF : (z + 1) * HALF, pl.ds(lane, n * 128)] for z in range(3)]

                return load

            base = half * PATCH + c * TILES * 2
            flow_chunk([loader(0), loader(1)], base, down, across, back, up, u_high, u_low, u_edge, g_edge, stat, advance)

        return carry

    lax.fori_loop(0, 2 * CHUNKS, one, 0)
    for half in range(2):
        for r in range(2):
            for k, row in enumerate(flow_rows(stat, half * 128 + r * HALF, half)):
                out[half, k, pl.ds(r, 1), :] = row

    @pl.when(gives(0))
    def _():
        strip(0, CHUNKS, 128).wait_send()

    @pl.when(both(works(0), above))
    def _():
        halo(0, CHUNKS, 128).wait_send()
        relay(0, CHUNKS, 128).wait_send()

    def end(i, carry):
        half, c = step(i)

        @pl.when(both(gives(half), jnp.logical_not(around(half, c))))
        def _():
            strip(half, c).wait_send()

        @pl.when(around(half, c))
        def _():
            detour(half, c).wait_send()

        @pl.when(passes(half, c))
        def _():
            onward(half, c).wait_send()

        @pl.when(both(works(half), above))
        def _():
            halo(half, c).wait_send()
            relay(half, c).wait_send()

        return carry

    lax.fori_loop(0, 2 * CHUNKS, end, 0)


def flow_of(x):
    vmem = pl.BlockSpec(memory_space=pltpu.VMEM)
    wide = (TILES + 1) * 128
    dma = pltpu.SemaphoreType.DMA
    return pl.pallas_call(
        flow_kernel,
        out_shape=jax.ShapeDtypeStruct((2, 2, 2, 128), f32),
        in_specs=[pl.BlockSpec(memory_space=pl.ANY)] + [vmem] * 4,
        out_specs=vmem,
        scratch_shapes=[
            pltpu.VMEM((2, PATCH + HALF, 2 * SIDE * 128), f32),
            pltpu.VMEM((2, 2, 128, wide), bf16),
            pltpu.VMEM((2, 2, 128, wide), bf16),
            pltpu.VMEM((2, 2, 8, wide), f32),
            pltpu.VMEM((TILES * 4, 128), f32),
            pltpu.VMEM((3, 256, 8, 128), f32),
            dma((2,)),
        ]
        + [dma((2, CHUNKS + 1))] * 6,
        compiler_params=pltpu.CompilerParams(vmem_limit_bytes=56 << 20, collective_id=0, has_side_effects=True),
    )(x, *(jnp.asarray(t) for t in tables()))


def relax_kernel(pieces, masks, carried, flow_out, aligned_out, mine, blocks, result, sec_send, sec_recv, tile_send, tile_recv):
    sec, tile = lax.axis_index("sec"), lax.axis_index("tile")
    secs, tiles = lax.axis_size("sec"), lax.axis_size("tile")
    barrier = pltpu.get_barrier_semaphore()
    steps = (1, 2, tiles - 1, tiles - 2)
    slots = (1, 0, 3, 4)
    for k in range(1, secs):
        pl.semaphore_signal(barrier, inc=1, device_id=(lax.rem(sec + k, secs), tile), device_id_type=MESH)
    for k in steps:
        pl.semaphore_signal(barrier, inc=1, device_id=(sec, lax.rem(tile + k, tiles)), device_id_type=MESH)
    rows = [pieces[h, k] for h in range(2) for k in range(2)]
    rows += [masks[...].astype(f32), carried[0], carried[1], jnp.zeros((2, 128), f32)]
    mine[pl.ds(sec, 1)] = jnp.concatenate(rows, 0)[None]
    pl.semaphore_wait(barrier, secs - 1 + len(steps))

    def to_sec(k, owner):
        return pltpu.make_async_remote_copy(
            mine.at[owner],
            mine.at[owner],
            sec_send.at[k],
            sec_recv.at[k],
            device_id=(lax.rem(sec + k, secs), tile),
            device_id_type=MESH,
        )

    for k in range(1, secs):
        to_sec(k, sec).start()
    for k in range(1, secs):
        to_sec(k, lax.rem(sec + secs - k, secs)).wait_recv()
    for s in range(secs):
        whole = mine[0, 10:14] if s == 0 else mine[s, 0:4] + mine[s - 1, 4:8]
        blocks[2, s] = jnp.concatenate([whole, mine[s, 8:10], jnp.zeros((2, 128), f32)], 0)
    copies = [
        pltpu.make_async_remote_copy(
            blocks.at[2],
            blocks.at[slot],
            tile_send.at[n],
            tile_recv.at[n],
            device_id=(sec, lax.rem(tile + k, tiles)),
            device_id_type=MESH,
        )
        for n, (k, slot) in enumerate(zip(steps, slots))
    ]
    for copy in copies:
        copy.start()
    for copy in copies:
        copy.wait_recv()

    def window(get):
        return jnp.concatenate([get(0)[1:2], get(1), get(2), get(3), get(4)[0:1]], 0)

    flow = [[window(lambda d: blocks[d, s, 2 * k : 2 * k + 2]) for k in range(2)] for s in range(secs)]
    zero = jnp.zeros((8, 128), f32)
    pairs = [zero] + [link_weight * window(lambda d: blocks[d, s, 4:6]) for s in range(1, secs)] + [zero]
    node = 2 * tile - 3 + lax.broadcasted_iota(jnp.int32, (8, 128), 0)
    column = lax.broadcasted_iota(jnp.int32, (8, 128), 1)
    last = 2 * tiles - 1
    inside = jnp.logical_and(node >= 0, node <= last)
    at_left, at_right = column == 0, column == 127

    def as_float(test):
        return jnp.where(test, 1.0, 0.0)

    degree = 4.0 - as_float(node == 0) - as_float(node == last) - as_float(at_left) - as_float(at_right)
    start = [[jnp.where(inside, v, 0.0) for v in flow[0]]]
    for s in range(1, secs):
        start.append([start[s - 1][k] + jnp.where(inside, flow[s][k], 0.0) for k in range(2)])
    inverse = [
        jnp.where(inside, 1.0 / (spring_weight * degree + pairs[s] + pairs[s + 1] + anchor_weight), 0.0)
        for s in range(secs)
    ]
    fixed = []
    for s in range(secs):
        row = []
        for k in range(2):
            v = anchor_weight * start[s][k]
            if s > 0:
                v = v + pairs[s] * flow[s][k]
            if s + 1 < secs:
                v = v - pairs[s + 1] * flow[s + 1][k]
            row.append(v)
        fixed.append(row)
    aligned = start
    for step in range(ITERS):
        new = []
        for s in range(secs):
            row = []
            for k in range(2):
                v = aligned[s][k]
                total = fixed[s][k] + spring_weight * (
                    pltpu.roll(v, 1, 0)
                    + pltpu.roll(v, 7, 0)
                    + jnp.where(at_left, 0.0, pltpu.roll(v, 1, 1))
                    + jnp.where(at_right, 0.0, pltpu.roll(v, 127, 1))
                )
                if s > 0:
                    total = total + pairs[s] * aligned[s - 1][k]
                if s + 1 < secs:
                    total = total + pairs[s + 1] * aligned[s + 1][k]
                row.append(jnp.where(inside, total * inverse[s], 0.0))
            new.append(row)
        aligned = new
    for s in range(secs):
        for k in range(2):
            result[s, k] = flow[s][k]
            result[s, 2 + k] = aligned[s][k]
    for k in range(2):
        flow_out[k] = result[sec, k][3:5]
        aligned_out[k] = result[sec, 2 + k][3:5]
    for k in range(1, secs):
        to_sec(k, sec).wait_send()
    for copy in copies:
        copy.wait_send()


def relaxed(pieces, masks, carried):
    vmem = pl.BlockSpec(memory_space=pltpu.VMEM)
    dma = pltpu.SemaphoreType.DMA
    secs = lax.axis_size("sec")
    shape = jax.ShapeDtypeStruct((2, 2, 128), f32)
    return pl.pallas_call(
        relax_kernel,
        out_shape=(shape, shape),
        in_specs=[vmem] * 3,
        out_specs=(vmem, vmem),
        scratch_shapes=[
            pltpu.VMEM((secs, 16, 128), f32),
            pltpu.VMEM((5, secs, 8, 128), f32),
            pltpu.VMEM((secs, 4, 8, 128), f32),
            dma((secs,)),
            dma((secs,)),
            dma((4,)),
            dma((4,)),
        ],
        compiler_params=pltpu.CompilerParams(collective_id=1, has_side_effects=True),
    )(pieces, masks, carried)


def shards(sections, masks, carried):
    flow, aligned = relaxed(flow_of(sections[0]), masks[0], carried)
    return flow[None], aligned[None]


def solution(mesh):
    in_specs = (P("sec", "tile", None), P("sec", "tile", None), P(None, "tile", None))
    out_specs = (P("sec", None, "tile", None), P("sec", None, "tile", None))
    return jax.shard_map(shards, mesh=mesh, in_specs=in_specs, out_specs=out_specs, check_vma=False)
```

```python
import math

import jax
import jax.numpy as jnp
import ml_dtypes
import numpy as np
from jax import lax
from jax.experimental import pallas as pl
from jax.experimental.pallas import tpu as pltpu
from jax.sharding import PartitionSpec as P

COLS = 8192
PATCH = 128
STRIDE = 64
ITERS = 3
HALF = PATCH // 2
TILES = 8
QUAD = 8
SIDE = 33
CHUNKS = 4
DETOUR = 4
MESH = pl.DeviceIdType.MESH

spring_weight = 1.0
link_weight = 4.0
anchor_weight = 0.5
bf16 = jnp.bfloat16
f32 = jnp.float32


def two_terms(table):
    table = table.astype(np.float32)
    high = table.astype(ml_dtypes.bfloat16)
    low = (table - high.astype(np.float32)).astype(ml_dtypes.bfloat16)
    return high, low


def tables():
    index = np.arange(PATCH)
    phase = np.outer(index, index) % PATCH
    cosine = np.cos(2 * np.pi * phase / PATCH)
    sine = np.sin(2 * np.pi * phase / PATCH)
    down = np.zeros((PATCH + 16, PATCH))
    down[:HALF] = cosine[:HALF]
    down[HALF:PATCH] = sine[:HALF]
    down[PATCH:] = cosine[HALF]
    high, low = two_terms(down)
    down = np.concatenate([high, high, low], 1)
    high, low = two_terms(np.block([[cosine, -sine], [-sine, -cosine]]))
    across = np.concatenate([high, high, low], 0)
    high, low = two_terms(np.block([[cosine, sine], [-sine, cosine]]))
    back = np.concatenate([high, high, low], 0)
    share = np.full(HALF, 2.0)
    share[0] = 1.0
    up = np.concatenate([cosine[:, :HALF] * share, -sine[:, :HALF] * share], 1)
    up[:, HALF] = cosine[:, HALF]
    high, low = two_terms(up * (math.log2(math.e) / PATCH**3))
    up = np.concatenate([high, high, low], 1)
    return down, across, back, up


def split(value):
    high = value.astype(bf16)
    return high, (value - high.astype(f32)).astype(bf16)


def dot(left, right):
    return lax.dot_general(left, right, (((1,), (0,)), ((), ())), preferred_element_type=f32)


def three(value, axis):
    high, low = split(value)
    return jnp.concatenate([high, low, high], axis)


def cross(spec, count):
    ar, ai = spec[:count, :PATCH], spec[:count, PATCH:]
    br, bi = spec[count:, :PATCH], spec[count:, PATCH:]
    return three(jnp.concatenate([ar * br + ai * bi, ar * bi - ai * br], 1), 1)


def flow_chunk(loads, base, down, across, back, up, u_high, u_low, u_edge, g_edge, stat):
    for s in range(2):
        for tile in range(0, TILES + 1, 2):
            n = min(2, TILES + 1 - tile)
            top, mid, halo = [split(cell) for cell in loads[s](tile, n)]
            for r, first in ((0, top), (1, halo)):
                right = jnp.concatenate([first[0], mid[0], first[1], mid[1], first[0], mid[0]], 0)
                u = dot(down[...], right)
                high, low = split(u[:PATCH])
                lanes = slice(tile * 128, (tile + n) * 128)
                u_high[s, r, :, lanes] = high
                u_low[s, r, :, lanes] = low
                u_edge[s, r, :, lanes] = u[PATCH : PATCH + 8]
    left_lanes = lax.broadcasted_iota(jnp.int32, (HALF, 128), 1) < HALF
    left_lanes8 = lax.broadcasted_iota(jnp.int32, (8, 128), 1) < HALF
    sub8 = lax.broadcasted_iota(jnp.int32, (8, 128), 0)
    count = TILES * 4
    blocks = []
    for s in range(2):
        for group in range(count // 8):
            rows = jnp.zeros((8, 128), f32)
            for k in range(8):
                p = group * 8 + k
                tile, parity, r = p // 4, (p // 2) % 2, p % 2
                window = u_edge[s, r, :, tile * 128 : (tile + 1) * 128]
                if parity:
                    window = jnp.where(left_lanes8, u_edge[s, r, :, (tile + 1) * 128 : (tile + 2) * 128], window)
                rows = jnp.where(sub8 == k, window, rows)
            blocks.append(rows)
    real_rows = jnp.concatenate([across[i * 256 : i * 256 + 128] for i in range(3)], 0)
    spec = dot(three(jnp.concatenate(blocks, 0), 1), real_rows)
    g_edge[...] = dot(cross(spec, count), back[...])[:, :128]

    def some(i, carry):
        left = []
        for s in range(2):
            for q in range(QUAD):
                lane = pl.multiple_of((i * QUAD + q) * 128, 128)
                for parity in range(2):
                    for r in range(2):
                        parts = []
                        for ref in (u_high, u_low):
                            for half in range(2):
                                rows = slice(half * HALF, (half + 1) * HALF)
                                window = ref[s, r, rows, pl.ds(lane, 128)]
                                if parity:
                                    window = jnp.where(left_lanes, ref[s, r, rows, pl.ds(lane + 128, 128)], window)
                                parts.append(window)
                        left.append(jnp.concatenate(parts + parts[:2], 1))
        spec = dot(jnp.concatenate(left, 0), across[...])
        g = dot(cross(spec, QUAD * 4 * HALF), back[...])
        for j in range(QUAD * 2):
            columns = []
            for r in range(2):
                p = j * 2 + r
                real = g[p * HALF : (p + 1) * HALF, :128]
                imag = g[p * HALF : (p + 1) * HALF, 128:]
                edge = g_edge[pl.ds(i * QUAD * 4 + p, 1), :]
                first = jnp.where(sub8 == 0, jnp.broadcast_to(edge, (8, 128)), imag[:8])
                columns.append(jnp.concatenate([real, first, imag[8:]], 0))
            scores = dot(up[...], three(jnp.concatenate(columns, 1), 0))
            for r in range(2):
                part = [scores[k * 8 : (k + 1) * 8, r * 128 : (r + 1) * 128] for k in range(16)]
                tops = part
                while len(tops) > 1:
                    tops = [jnp.maximum(tops[2 * z], tops[2 * z + 1]) for z in range(len(tops) // 2)]
                expo = [jnp.exp2(k - tops[0]) for k in part]
                plus, plus_rows = expo[7], expo[7]
                for k in range(6, 0, -1):
                    plus = plus + expo[k]
                    plus_rows = plus_rows + plus
                plus = plus + expo[0]
                minus, minus_rows = expo[8], expo[8]
                for k in range(9, 16):
                    minus = minus + expo[k]
                    minus_rows = minus_rows + minus
                at = base + r * HALF + i * QUAD * 2 + j
                stat[0, pl.ds(at, 1)] = tops[0][None]
                stat[1, pl.ds(at, 1)] = (plus + minus)[None]
                stat[2, pl.ds(at, 1)] = (plus_rows - minus_rows)[None]
        return carry

    lax.fori_loop(0, TILES // QUAD, some, 0)


def flow_rows(stat, at, half):
    top, total, rows = (stat[k, pl.ds(at, HALF)] for k in range(3))
    most = jnp.max(jnp.max(top, axis=1, keepdims=True), axis=2, keepdims=True)
    scale = jnp.exp2(top - most)
    sub = lax.broadcasted_iota(jnp.int32, (1, 8, 128), 1).astype(f32)
    total = total * scale
    rows = jnp.sum(rows * scale * 8.0 + total * sub, axis=1)
    total = jnp.sum(total, axis=1)
    lane = lax.broadcasted_iota(jnp.int32, (HALF, 128), 1)
    wrapped = jnp.where(lane >= HALF, lane - PATCH, lane).astype(f32)
    columns = jnp.sum(total * wrapped, axis=1, keepdims=True)
    rows = jnp.sum(rows, axis=1, keepdims=True)
    total = jnp.sum(total, axis=1, keepdims=True)
    here = lane == lax.broadcasted_iota(jnp.int32, (HALF, 128), 0) + half * HALF
    return [
        jnp.sum(jnp.where(here, jnp.broadcast_to(v / total, (HALF, 128)), 0.0), axis=0, keepdims=True)
        for v in (rows, columns)
    ]


def flow_kernel(x, down, across, back, up, out, strips, u_high, u_low, u_edge, g_edge, stat,
                own_sem, strip_send, strip_recv, halo_send, halo_recv, relay_send, relay_recv):
    sec, tile = lax.axis_index("sec"), lax.axis_index("tile")
    secs, tiles = lax.axis_size("sec"), lax.axis_size("tile")
    barrier = pltpu.get_barrier_semaphore()
    for place in (
        (lax.rem(sec + 1, secs), tile),
        (lax.rem(sec + secs - 1, secs), tile),
        (sec, lax.rem(tile + 1, tiles)),
        (sec, lax.rem(tile + tiles - 1, tiles)),
    ):
        pl.semaphore_signal(barrier, inc=1, device_id=place, device_id_type=MESH)
    swapped = tile + 2 - 4 * lax.rem(tile // 2, 2)
    first, last = sec == 0, sec == secs - 1
    middle = secs // 2
    lower, upper = sec == middle - 1, sec == middle

    @pl.when(jnp.logical_or(first, last))
    def _():
        for there in (middle - 1, middle):
            pl.semaphore_signal(barrier, inc=1, device_id=(there, swapped), device_id_type=MESH)

    @pl.when(jnp.logical_or(lower, upper))
    def _():
        for there in (0, secs - 1):
            pl.semaphore_signal(barrier, inc=1, device_id=(there, swapped), device_id_type=MESH)

    width = TILES * 128

    def own(half):
        first, n = (0, SIDE) if half == 0 else (SIDE - 1, SIDE - 1)
        return pltpu.make_async_copy(
            x.at[:, pl.ds(first * 128, n * 128)],
            strips.at[1 - half, pl.ds(0, PATCH), pl.ds(half * SIDE * 128, n * 128)],
            own_sem.at[half],
        )

    for half in range(2):
        own(half).start()
    outer = jnp.logical_or(jnp.logical_or(first, last), jnp.logical_or(lower, upper))
    pl.semaphore_wait(barrier, jnp.where(outer, 6, 4))

    def spans(half, c, n):
        source = pl.multiple_of((half * (SIDE - 1) + c * TILES) * 128, 128)
        target = pl.multiple_of((half * SIDE + c * TILES) * 128, 128)
        return pl.ds(source, n), pl.ds(target, n)

    def strip(half, c, n=width):
        source, target = spans(half, c, n)
        return pltpu.make_async_remote_copy(
            x.at[:, source],
            strips.at[half, pl.ds(0, PATCH), target],
            strip_send.at[half, c],
            strip_recv.at[half, c],
            device_id=(lax.rem(sec + 1 - 2 * half + secs, secs), tile),
            device_id_type=MESH,
        )

    def detour(half, c):
        source, _ = spans(half, c, width)
        _, target = spans(1 - half, c, width)
        return pltpu.make_async_remote_copy(
            x.at[:, source],
            strips.at[1 - half, pl.ds(0, PATCH), target],
            strip_send.at[half, c],
            strip_recv.at[1 - half, c],
            device_id=((secs - 1) * (1 - half), swapped),
            device_id_type=MESH,
        )

    def onward(half, c):
        _, source = spans(half, c, width)
        _, target = spans(1 - half, c, width)
        return pltpu.make_async_remote_copy(
            strips.at[half, pl.ds(0, PATCH), source],
            strips.at[1 - half, pl.ds(0, PATCH), target],
            strip_send.at[1 - half, c],
            strip_recv.at[1 - half, c],
            device_id=(middle - 1 + half, swapped),
            device_id_type=MESH,
        )

    def around(half, c):
        mine = jnp.logical_or(jnp.logical_and(half == 0, lower), jnp.logical_and(half == 1, upper))
        return jnp.logical_and(mine, c < DETOUR)

    def passes(half, c):
        mine = jnp.logical_or(jnp.logical_and(half == 0, first), jnp.logical_and(half == 1, last))
        return jnp.logical_and(mine, c < DETOUR)

    def halo(half, c, n=width):
        source, target = spans(half, c, n)
        return pltpu.make_async_remote_copy(
            x.at[pl.ds(0, HALF), source],
            strips.at[1 - half, pl.ds(PATCH, HALF), target],
            halo_send.at[half, c],
            halo_recv.at[half, c],
            device_id=(sec, lax.rem(tile + tiles - 1, tiles)),
            device_id_type=MESH,
        )

    def relay(half, c, n=width):
        _, target = spans(half, c, n)
        return pltpu.make_async_remote_copy(
            strips.at[half, pl.ds(0, HALF), target],
            strips.at[half, pl.ds(PATCH, HALF), target],
            relay_send.at[half, c],
            relay_recv.at[half, c],
            device_id=(sec, lax.rem(tile + tiles - 1, tiles)),
            device_id_type=MESH,
        )

    def gives(half):
        return jnp.logical_or(jnp.logical_and(half == 0, sec < secs - 1), jnp.logical_and(half == 1, sec > 0))

    def works(half):
        return jnp.logical_or(jnp.logical_and(half == 0, sec > 0), jnp.logical_and(half == 1, sec < secs - 1))

    above, under = tile > 0, tile < tiles - 1

    def both(p, q):
        return jnp.logical_and(p, q)

    def step(i):
        apart = jnp.logical_or(lower, upper)
        half = lax.rem(jnp.where(apart, i // CHUNKS, i) + jnp.where(jnp.logical_or(upper, last), 1, 0), 2)
        return half, CHUNKS - 1 - jnp.where(apart, lax.rem(i, CHUNKS), i // 2)

    @pl.when(gives(0))
    def _():
        strip(0, CHUNKS, 128).start()

    @pl.when(both(works(0), above))
    def _():
        halo(0, CHUNKS, 128).start()

    def begin(i, carry):
        half, c = step(i)

        @pl.when(both(gives(half), jnp.logical_not(around(half, c))))
        def _():
            strip(half, c).start()

        @pl.when(around(half, c))
        def _():
            detour(half, c).start()

        @pl.when(both(works(half), above))
        def _():
            halo(half, c).start()

        return carry

    lax.fori_loop(0, 2 * CHUNKS, begin, 0)
    for s in range(2):
        strips[s, :, (2 * SIDE - 1) * 128 :] = jnp.zeros((PATCH + HALF, 128), f32)

    @pl.when(jnp.logical_not(under))
    def _():
        for s in range(2):
            strips[s, PATCH:, : (2 * SIDE - 1) * 128] = jnp.zeros((HALF, (2 * SIDE - 1) * 128), f32)

    for half in range(2):
        own(half).wait()

    @pl.when(works(0))
    def _():
        strip(0, CHUNKS, 128).wait_recv()

        @pl.when(above)
        def _():
            relay(0, CHUNKS, 128).start()

    def arrive(half, c):
        @pl.when(works(half))
        def _():
            strip(half, c).wait_recv()

            @pl.when(above)
            def _():
                relay(half, c).start()

        @pl.when(passes(half, c))
        def _():
            detour(1 - half, c).wait_recv()
            onward(half, c).start()

    arrive(*step(0))

    @pl.when(both(works(0), under))
    def _():
        halo(0, CHUNKS, 128).wait_recv()
        relay(0, CHUNKS, 128).wait_recv()

    def one(i, carry):
        half, c = step(i)

        @pl.when(i + 1 < 2 * CHUNKS)
        def _():
            arrive(*step(i + 1))

        @pl.when(works(half))
        def _():
            @pl.when(under)
            def _():
                halo(half, c).wait_recv()
                relay(half, c).wait_recv()

            def loader(s):
                def load(tile, n):
                    lane = pl.multiple_of((half * SIDE + c * TILES + tile) * 128, 128)
                    return [strips[s, z * HALF : (z + 1) * HALF, pl.ds(lane, n * 128)] for z in range(3)]

                return load

            base = half * PATCH + c * TILES * 2
            flow_chunk([loader(0), loader(1)], base, down, across, back, up, u_high, u_low, u_edge, g_edge, stat)

        return carry

    lax.fori_loop(0, 2 * CHUNKS, one, 0)
    for half in range(2):
        for r in range(2):
            for k, row in enumerate(flow_rows(stat, half * 128 + r * HALF, half)):
                out[half, k, pl.ds(r, 1), :] = row

    @pl.when(gives(0))
    def _():
        strip(0, CHUNKS, 128).wait_send()

    @pl.when(both(works(0), above))
    def _():
        halo(0, CHUNKS, 128).wait_send()
        relay(0, CHUNKS, 128).wait_send()

    def end(i, carry):
        half, c = step(i)

        @pl.when(both(gives(half), jnp.logical_not(around(half, c))))
        def _():
            strip(half, c).wait_send()

        @pl.when(around(half, c))
        def _():
            detour(half, c).wait_send()

        @pl.when(passes(half, c))
        def _():
            onward(half, c).wait_send()

        @pl.when(both(works(half), above))
        def _():
            halo(half, c).wait_send()
            relay(half, c).wait_send()

        return carry

    lax.fori_loop(0, 2 * CHUNKS, end, 0)


def flow_of(x):
    vmem = pl.BlockSpec(memory_space=pltpu.VMEM)
    wide = (TILES + 1) * 128
    dma = pltpu.SemaphoreType.DMA
    return pl.pallas_call(
        flow_kernel,
        out_shape=jax.ShapeDtypeStruct((2, 2, 2, 128), f32),
        in_specs=[pl.BlockSpec(memory_space=pl.ANY)] + [vmem] * 4,
        out_specs=vmem,
        scratch_shapes=[
            pltpu.VMEM((2, PATCH + HALF, 2 * SIDE * 128), f32),
            pltpu.VMEM((2, 2, 128, wide), bf16),
            pltpu.VMEM((2, 2, 128, wide), bf16),
            pltpu.VMEM((2, 2, 8, wide), f32),
            pltpu.VMEM((TILES * 4, 128), f32),
            pltpu.VMEM((3, 256, 8, 128), f32),
            dma((2,)),
        ]
        + [dma((2, CHUNKS + 1))] * 6,
        compiler_params=pltpu.CompilerParams(vmem_limit_bytes=56 << 20, collective_id=0, has_side_effects=True),
    )(x, *(jnp.asarray(t) for t in tables()))


def relax_kernel(pieces, masks, carried, flow_out, aligned_out, mine, blocks, result, sec_send, sec_recv, tile_send, tile_recv):
    sec, tile = lax.axis_index("sec"), lax.axis_index("tile")
    secs, tiles = lax.axis_size("sec"), lax.axis_size("tile")
    barrier = pltpu.get_barrier_semaphore()
    steps = (1, 2, tiles - 1, tiles - 2)
    slots = (1, 0, 3, 4)
    for k in range(1, secs):
        pl.semaphore_signal(barrier, inc=1, device_id=(lax.rem(sec + k, secs), tile), device_id_type=MESH)
    for k in steps:
        pl.semaphore_signal(barrier, inc=1, device_id=(sec, lax.rem(tile + k, tiles)), device_id_type=MESH)
    rows = [pieces[h, k] for h in range(2) for k in range(2)]
    rows += [masks[...].astype(f32), carried[0], carried[1], jnp.zeros((2, 128), f32)]
    mine[pl.ds(sec, 1)] = jnp.concatenate(rows, 0)[None]
    pl.semaphore_wait(barrier, secs - 1 + len(steps))

    def to_sec(k, owner):
        return pltpu.make_async_remote_copy(
            mine.at[owner],
            mine.at[owner],
            sec_send.at[k],
            sec_recv.at[k],
            device_id=(lax.rem(sec + k, secs), tile),
            device_id_type=MESH,
        )

    for k in range(1, secs):
        to_sec(k, sec).start()
    for k in range(1, secs):
        to_sec(k, lax.rem(sec + secs - k, secs)).wait_recv()
    for s in range(secs):
        whole = mine[0, 10:14] if s == 0 else mine[s, 0:4] + mine[s - 1, 4:8]
        blocks[2, s] = jnp.concatenate([whole, mine[s, 8:10], jnp.zeros((2, 128), f32)], 0)
    copies = [
        pltpu.make_async_remote_copy(
            blocks.at[2],
            blocks.at[slot],
            tile_send.at[n],
            tile_recv.at[n],
            device_id=(sec, lax.rem(tile + k, tiles)),
            device_id_type=MESH,
        )
        for n, (k, slot) in enumerate(zip(steps, slots))
    ]
    for copy in copies:
        copy.start()
    for copy in copies:
        copy.wait_recv()

    def window(get):
        return jnp.concatenate([get(0)[1:2], get(1), get(2), get(3), get(4)[0:1]], 0)

    flow = [[window(lambda d: blocks[d, s, 2 * k : 2 * k + 2]) for k in range(2)] for s in range(secs)]
    zero = jnp.zeros((8, 128), f32)
    pairs = [zero] + [link_weight * window(lambda d: blocks[d, s, 4:6]) for s in range(1, secs)] + [zero]
    node = 2 * tile - 3 + lax.broadcasted_iota(jnp.int32, (8, 128), 0)
    column = lax.broadcasted_iota(jnp.int32, (8, 128), 1)
    last = 2 * tiles - 1
    inside = jnp.logical_and(node >= 0, node <= last)
    at_left, at_right = column == 0, column == 127

    def as_float(test):
        return jnp.where(test, 1.0, 0.0)

    degree = 4.0 - as_float(node == 0) - as_float(node == last) - as_float(at_left) - as_float(at_right)
    start = [[jnp.where(inside, v, 0.0) for v in flow[0]]]
    for s in range(1, secs):
        start.append([start[s - 1][k] + jnp.where(inside, flow[s][k], 0.0) for k in range(2)])
    inverse = [
        jnp.where(inside, 1.0 / (spring_weight * degree + pairs[s] + pairs[s + 1] + anchor_weight), 0.0)
        for s in range(secs)
    ]
    fixed = []
    for s in range(secs):
        row = []
        for k in range(2):
            v = anchor_weight * start[s][k]
            if s > 0:
                v = v + pairs[s] * flow[s][k]
            if s + 1 < secs:
                v = v - pairs[s + 1] * flow[s + 1][k]
            row.append(v)
        fixed.append(row)
    aligned = start
    for step in range(ITERS):
        new = []
        for s in range(secs):
            row = []
            for k in range(2):
                v = aligned[s][k]
                total = fixed[s][k] + spring_weight * (
                    pltpu.roll(v, 1, 0)
                    + pltpu.roll(v, 7, 0)
                    + jnp.where(at_left, 0.0, pltpu.roll(v, 1, 1))
                    + jnp.where(at_right, 0.0, pltpu.roll(v, 127, 1))
                )
                if s > 0:
                    total = total + pairs[s] * aligned[s - 1][k]
                if s + 1 < secs:
                    total = total + pairs[s + 1] * aligned[s + 1][k]
                row.append(jnp.where(inside, total * inverse[s], 0.0))
            new.append(row)
        aligned = new
    for s in range(secs):
        for k in range(2):
            result[s, k] = flow[s][k]
            result[s, 2 + k] = aligned[s][k]
    for k in range(2):
        flow_out[k] = result[sec, k][3:5]
        aligned_out[k] = result[sec, 2 + k][3:5]
    for k in range(1, secs):
        to_sec(k, sec).wait_send()
    for copy in copies:
        copy.wait_send()


def relaxed(pieces, masks, carried):
    vmem = pl.BlockSpec(memory_space=pltpu.VMEM)
    dma = pltpu.SemaphoreType.DMA
    secs = lax.axis_size("sec")
    shape = jax.ShapeDtypeStruct((2, 2, 128), f32)
    return pl.pallas_call(
        relax_kernel,
        out_shape=(shape, shape),
        in_specs=[vmem] * 3,
        out_specs=(vmem, vmem),
        scratch_shapes=[
            pltpu.VMEM((secs, 16, 128), f32),
            pltpu.VMEM((5, secs, 8, 128), f32),
            pltpu.VMEM((secs, 4, 8, 128), f32),
            dma((secs,)),
            dma((secs,)),
            dma((4,)),
            dma((4,)),
        ],
        compiler_params=pltpu.CompilerParams(collective_id=1, has_side_effects=True),
    )(pieces, masks, carried)


def shards(sections, masks, carried):
    flow, aligned = relaxed(flow_of(sections[0]), masks[0], carried)
    return flow[None], aligned[None]


def solution(mesh):
    in_specs = (P("sec", "tile", None), P("sec", "tile", None), P(None, "tile", None))
    out_specs = (P("sec", None, "tile", None), P("sec", None, "tile", None))
    return jax.shard_map(shards, mesh=mesh, in_specs=in_specs, out_specs=out_specs, check_vma=False)
```

```python
import math

import jax
import jax.numpy as jnp
import ml_dtypes
import numpy as np
from jax import lax
from jax.experimental import pallas as pl
from jax.experimental.pallas import tpu as pltpu
from jax.sharding import PartitionSpec as P

COLS = 8192
PATCH = 128
STRIDE = 64
ITERS = 3
HALF = PATCH // 2
TILES = 8
QUAD = 8
SIDE = 33
CHUNKS = 4
DETOUR = 4
MESH = pl.DeviceIdType.MESH

spring_weight = 1.0
link_weight = 4.0
anchor_weight = 0.5
bf16 = jnp.bfloat16
f32 = jnp.float32


def two_terms(table):
    table = table.astype(np.float32)
    high = table.astype(ml_dtypes.bfloat16)
    low = (table - high.astype(np.float32)).astype(ml_dtypes.bfloat16)
    return high, low


def tables():
    index = np.arange(PATCH)
    phase = np.outer(index, index) % PATCH
    cosine = np.cos(2 * np.pi * phase / PATCH)
    sine = np.sin(2 * np.pi * phase / PATCH)
    down = np.zeros((PATCH + 16, PATCH))
    down[:HALF] = cosine[:HALF]
    down[HALF:PATCH] = sine[:HALF]
    down[PATCH:] = cosine[HALF]
    high, low = two_terms(down)
    down = np.concatenate([high, high, low], 1)
    high, low = two_terms(np.block([[cosine, -sine], [-sine, -cosine]]))
    across = np.concatenate([high, high, low], 0)
    high, low = two_terms(np.block([[cosine, sine], [-sine, cosine]]))
    back = np.concatenate([high, high, low], 0)
    share = np.full(HALF, 2.0)
    share[0] = 1.0
    up = np.concatenate([cosine[:, :HALF] * share, -sine[:, :HALF] * share], 1)
    up[:, HALF] = cosine[:, HALF]
    high, low = two_terms(up * (math.log2(math.e) / PATCH**3))
    up = np.concatenate([high, high, low], 1)
    return down, across, back, up


def split(value):
    high = value.astype(bf16)
    return high, (value - high.astype(f32)).astype(bf16)


def dot(left, right):
    return lax.dot_general(left, right, (((1,), (0,)), ((), ())), preferred_element_type=f32)


def three(value, axis):
    high, low = split(value)
    return jnp.concatenate([high, low, high], axis)


def cross(spec, count):
    ar, ai = spec[:count, :PATCH], spec[:count, PATCH:]
    br, bi = spec[count:, :PATCH], spec[count:, PATCH:]
    return three(jnp.concatenate([ar * br + ai * bi, ar * bi - ai * br], 1), 1)


def flow_chunk(loads, base, down, across, back, up, u_high, u_low, u_edge, g_edge, stat):
    for s in range(2):
        for tile in range(0, TILES + 1, 2):
            n = min(2, TILES + 1 - tile)
            top, mid, halo = [split(cell) for cell in loads[s](tile, n)]
            for r, first in ((0, top), (1, halo)):
                right = jnp.concatenate([first[0], mid[0], first[1], mid[1], first[0], mid[0]], 0)
                u = dot(down[...], right)
                high, low = split(u[:PATCH])
                lanes = slice(tile * 128, (tile + n) * 128)
                u_high[s, r, :, lanes] = high
                u_low[s, r, :, lanes] = low
                u_edge[s, r, :, lanes] = u[PATCH : PATCH + 8]
    left_lanes = lax.broadcasted_iota(jnp.int32, (HALF, 128), 1) < HALF
    left_lanes8 = lax.broadcasted_iota(jnp.int32, (8, 128), 1) < HALF
    sub8 = lax.broadcasted_iota(jnp.int32, (8, 128), 0)
    count = TILES * 4
    blocks = []
    for s in range(2):
        for group in range(count // 8):
            rows = jnp.zeros((8, 128), f32)
            for k in range(8):
                p = group * 8 + k
                tile, parity, r = p // 4, (p // 2) % 2, p % 2
                window = u_edge[s, r, :, tile * 128 : (tile + 1) * 128]
                if parity:
                    window = jnp.where(left_lanes8, u_edge[s, r, :, (tile + 1) * 128 : (tile + 2) * 128], window)
                rows = jnp.where(sub8 == k, window, rows)
            blocks.append(rows)
    real_rows = jnp.concatenate([across[i * 256 : i * 256 + 128] for i in range(3)], 0)
    spec = dot(three(jnp.concatenate(blocks, 0), 1), real_rows)
    g_edge[...] = dot(cross(spec, count), back[...])[:, :128]

    def some(i, carry):
        left = []
        for s in range(2):
            for q in range(QUAD):
                lane = pl.multiple_of((i * QUAD + q) * 128, 128)
                for parity in range(2):
                    for r in range(2):
                        parts = []
                        for ref in (u_high, u_low):
                            for half in range(2):
                                rows = slice(half * HALF, (half + 1) * HALF)
                                window = ref[s, r, rows, pl.ds(lane, 128)]
                                if parity:
                                    window = jnp.where(left_lanes, ref[s, r, rows, pl.ds(lane + 128, 128)], window)
                                parts.append(window)
                        left.append(jnp.concatenate(parts + parts[:2], 1))
        spec = dot(jnp.concatenate(left, 0), across[...])
        g = dot(cross(spec, QUAD * 4 * HALF), back[...])
        for j in range(QUAD * 2):
            columns = []
            for r in range(2):
                p = j * 2 + r
                real = g[p * HALF : (p + 1) * HALF, :128]
                imag = g[p * HALF : (p + 1) * HALF, 128:]
                edge = g_edge[pl.ds(i * QUAD * 4 + p, 1), :]
                first = jnp.where(sub8 == 0, jnp.broadcast_to(edge, (8, 128)), imag[:8])
                columns.append(jnp.concatenate([real, first, imag[8:]], 0))
            scores = dot(up[...], three(jnp.concatenate(columns, 1), 0))
            for r in range(2):
                part = [scores[k * 8 : (k + 1) * 8, r * 128 : (r + 1) * 128] for k in range(16)]
                tops = part
                while len(tops) > 1:
                    tops = [jnp.maximum(tops[2 * z], tops[2 * z + 1]) for z in range(len(tops) // 2)]
                expo = [jnp.exp2(k - tops[0]) for k in part]
                plus, plus_rows = expo[7], expo[7]
                for k in range(6, 0, -1):
                    plus = plus + expo[k]
                    plus_rows = plus_rows + plus
                plus = plus + expo[0]
                minus, minus_rows = expo[8], expo[8]
                for k in range(9, 16):
                    minus = minus + expo[k]
                    minus_rows = minus_rows + minus
                at = base + r * HALF + i * QUAD * 2 + j
                stat[0, pl.ds(at, 1)] = tops[0][None]
                stat[1, pl.ds(at, 1)] = (plus + minus)[None]
                stat[2, pl.ds(at, 1)] = (plus_rows - minus_rows)[None]
        return carry

    lax.fori_loop(0, TILES // QUAD, some, 0)


def flow_rows(stat, at, half):
    top, total, rows = (stat[k, pl.ds(at, HALF)] for k in range(3))
    most = jnp.max(jnp.max(top, axis=1, keepdims=True), axis=2, keepdims=True)
    scale = jnp.exp2(top - most)
    sub = lax.broadcasted_iota(jnp.int32, (1, 8, 128), 1).astype(f32)
    total = total * scale
    rows = jnp.sum(rows * scale * 8.0 + total * sub, axis=1)
    total = jnp.sum(total, axis=1)
    lane = lax.broadcasted_iota(jnp.int32, (HALF, 128), 1)
    wrapped = jnp.where(lane >= HALF, lane - PATCH, lane).astype(f32)
    columns = jnp.sum(total * wrapped, axis=1, keepdims=True)
    rows = jnp.sum(rows, axis=1, keepdims=True)
    total = jnp.sum(total, axis=1, keepdims=True)
    here = lane == lax.broadcasted_iota(jnp.int32, (HALF, 128), 0) + half * HALF
    return [
        jnp.sum(jnp.where(here, jnp.broadcast_to(v / total, (HALF, 128)), 0.0), axis=0, keepdims=True)
        for v in (rows, columns)
    ]


def flow_kernel(x, down, across, back, up, out, strips, u_high, u_low, u_edge, g_edge, stat,
                own_sem, strip_send, strip_recv, halo_send, halo_recv, relay_send, relay_recv):
    sec, tile = lax.axis_index("sec"), lax.axis_index("tile")
    secs, tiles = lax.axis_size("sec"), lax.axis_size("tile")
    barrier = pltpu.get_barrier_semaphore()
    for place in (
        (lax.rem(sec + 1, secs), tile),
        (lax.rem(sec + secs - 1, secs), tile),
        (sec, lax.rem(tile + 1, tiles)),
        (sec, lax.rem(tile + tiles - 1, tiles)),
    ):
        pl.semaphore_signal(barrier, inc=1, device_id=place, device_id_type=MESH)
    swapped = tile + 2 - 4 * lax.rem(tile // 2, 2)
    first, last = sec == 0, sec == secs - 1
    middle = secs // 2
    lower, upper = sec == middle - 1, sec == middle

    @pl.when(jnp.logical_or(first, last))
    def _():
        for there in (middle - 1, middle):
            pl.semaphore_signal(barrier, inc=1, device_id=(there, swapped), device_id_type=MESH)

    @pl.when(jnp.logical_or(lower, upper))
    def _():
        for there in (0, secs - 1):
            pl.semaphore_signal(barrier, inc=1, device_id=(there, swapped), device_id_type=MESH)

    width = TILES * 128

    def own(half):
        first, n = (0, SIDE) if half == 0 else (SIDE - 1, SIDE - 1)
        return pltpu.make_async_copy(
            x.at[:, pl.ds(first * 128, n * 128)],
            strips.at[1 - half, pl.ds(0, PATCH), pl.ds(half * SIDE * 128, n * 128)],
            own_sem.at[half],
        )

    for half in range(2):
        own(half).start()
    outer = jnp.logical_or(jnp.logical_or(first, last), jnp.logical_or(lower, upper))
    pl.semaphore_wait(barrier, jnp.where(outer, 6, 4))

    def spans(half, c, n):
        source = pl.multiple_of((half * (SIDE - 1) + c * TILES) * 128, 128)
        target = pl.multiple_of((half * SIDE + c * TILES) * 128, 128)
        return pl.ds(source, n), pl.ds(target, n)

    def strip(half, c, n=width):
        source, target = spans(half, c, n)
        return pltpu.make_async_remote_copy(
            x.at[:, source],
            strips.at[half, pl.ds(0, PATCH), target],
            strip_send.at[half, c],
            strip_recv.at[half, c],
            device_id=(lax.rem(sec + 1 - 2 * half + secs, secs), tile),
            device_id_type=MESH,
        )

    def detour(half, c):
        source, _ = spans(half, c, width)
        _, target = spans(1 - half, c, width)
        return pltpu.make_async_remote_copy(
            x.at[:, source],
            strips.at[1 - half, pl.ds(0, PATCH), target],
            strip_send.at[half, c],
            strip_recv.at[1 - half, c],
            device_id=((secs - 1) * (1 - half), swapped),
            device_id_type=MESH,
        )

    def onward(half, c):
        _, source = spans(half, c, width)
        _, target = spans(1 - half, c, width)
        return pltpu.make_async_remote_copy(
            strips.at[half, pl.ds(0, PATCH), source],
            strips.at[1 - half, pl.ds(0, PATCH), target],
            strip_send.at[1 - half, c],
            strip_recv.at[1 - half, c],
            device_id=(middle - 1 + half, swapped),
            device_id_type=MESH,
        )

    def around(half, c):
        mine = jnp.logical_or(jnp.logical_and(half == 0, lower), jnp.logical_and(half == 1, upper))
        return jnp.logical_and(mine, c < DETOUR)

    def passes(half, c):
        mine = jnp.logical_or(jnp.logical_and(half == 0, first), jnp.logical_and(half == 1, last))
        return jnp.logical_and(mine, c < DETOUR)

    def halo(half, c, n=width):
        source, target = spans(half, c, n)
        return pltpu.make_async_remote_copy(
            x.at[pl.ds(0, HALF), source],
            strips.at[1 - half, pl.ds(PATCH, HALF), target],
            halo_send.at[half, c],
            halo_recv.at[half, c],
            device_id=(sec, lax.rem(tile + tiles - 1, tiles)),
            device_id_type=MESH,
        )

    def relay(half, c, n=width):
        _, target = spans(half, c, n)
        return pltpu.make_async_remote_copy(
            strips.at[half, pl.ds(0, HALF), target],
            strips.at[half, pl.ds(PATCH, HALF), target],
            relay_send.at[half, c],
            relay_recv.at[half, c],
            device_id=(sec, lax.rem(tile + tiles - 1, tiles)),
            device_id_type=MESH,
        )

    def gives(half):
        return jnp.logical_or(jnp.logical_and(half == 0, sec < secs - 1), jnp.logical_and(half == 1, sec > 0))

    def works(half):
        return jnp.logical_or(jnp.logical_and(half == 0, sec > 0), jnp.logical_and(half == 1, sec < secs - 1))

    above, under = tile > 0, tile < tiles - 1

    def both(p, q):
        return jnp.logical_and(p, q)

    def step(i):
        apart = jnp.logical_or(lower, upper)
        half = lax.rem(jnp.where(apart, i // CHUNKS, i) + jnp.where(jnp.logical_or(upper, last), 1, 0), 2)
        return half, CHUNKS - 1 - jnp.where(apart, lax.rem(i, CHUNKS), i // 2)

    @pl.when(gives(0))
    def _():
        strip(0, CHUNKS, 128).start()

    @pl.when(both(works(0), above))
    def _():
        halo(0, CHUNKS, 128).start()

    def begin(i, carry):
        half, c = step(i)

        @pl.when(both(gives(half), jnp.logical_not(around(half, c))))
        def _():
            strip(half, c).start()

        @pl.when(around(half, c))
        def _():
            detour(half, c).start()

        @pl.when(both(works(half), above))
        def _():
            halo(half, c).start()

        return carry

    lax.fori_loop(0, 2 * CHUNKS, begin, 0)
    for s in range(2):
        strips[s, :, (2 * SIDE - 1) * 128 :] = jnp.zeros((PATCH + HALF, 128), f32)

    @pl.when(jnp.logical_not(under))
    def _():
        for s in range(2):
            strips[s, PATCH:, : (2 * SIDE - 1) * 128] = jnp.zeros((HALF, (2 * SIDE - 1) * 128), f32)

    for half in range(2):
        own(half).wait()

    @pl.when(works(0))
    def _():
        strip(0, CHUNKS, 128).wait_recv()

        @pl.when(above)
        def _():
            relay(0, CHUNKS, 128).start()

    def arrive(half, c):
        @pl.when(works(half))
        def _():
            strip(half, c).wait_recv()

            @pl.when(above)
            def _():
                relay(half, c).start()

        @pl.when(passes(half, c))
        def _():
            detour(1 - half, c).wait_recv()
            onward(half, c).start()

    arrive(*step(0))

    @pl.when(both(works(0), under))
    def _():
        halo(0, CHUNKS, 128).wait_recv()
        relay(0, CHUNKS, 128).wait_recv()

    def one(i, carry):
        half, c = step(i)

        @pl.when(i + 1 < 2 * CHUNKS)
        def _():
            arrive(*step(i + 1))

        @pl.when(works(half))
        def _():
            @pl.when(under)
            def _():
                halo(half, c).wait_recv()
                relay(half, c).wait_recv()

            def loader(s):
                def load(tile, n):
                    lane = pl.multiple_of((half * SIDE + c * TILES + tile) * 128, 128)
                    return [strips[s, z * HALF : (z + 1) * HALF, pl.ds(lane, n * 128)] for z in range(3)]

                return load

            base = half * PATCH + c * TILES * 2
            flow_chunk([loader(0), loader(1)], base, down, across, back, up, u_high, u_low, u_edge, g_edge, stat)

        return carry

    lax.fori_loop(0, 2 * CHUNKS, one, 0)
    for half in range(2):
        for r in range(2):
            for k, row in enumerate(flow_rows(stat, half * 128 + r * HALF, half)):
                out[half, k, pl.ds(r, 1), :] = row

    @pl.when(gives(0))
    def _():
        strip(0, CHUNKS, 128).wait_send()

    @pl.when(both(works(0), above))
    def _():
        halo(0, CHUNKS, 128).wait_send()
        relay(0, CHUNKS, 128).wait_send()

    def end(i, carry):
        half, c = step(i)

        @pl.when(both(gives(half), jnp.logical_not(around(half, c))))
        def _():
            strip(half, c).wait_send()

        @pl.when(around(half, c))
        def _():
            detour(half, c).wait_send()

        @pl.when(passes(half, c))
        def _():
            onward(half, c).wait_send()

        @pl.when(both(works(half), above))
        def _():
            halo(half, c).wait_send()
            relay(half, c).wait_send()

        return carry

    lax.fori_loop(0, 2 * CHUNKS, end, 0)


def flow_of(x):
    vmem = pl.BlockSpec(memory_space=pltpu.VMEM)
    wide = (TILES + 1) * 128
    dma = pltpu.SemaphoreType.DMA
    return pl.pallas_call(
        flow_kernel,
        out_shape=jax.ShapeDtypeStruct((2, 2, 2, 128), f32),
        in_specs=[pl.BlockSpec(memory_space=pl.ANY)] + [vmem] * 4,
        out_specs=vmem,
        scratch_shapes=[
            pltpu.VMEM((2, PATCH + HALF, 2 * SIDE * 128), f32),
            pltpu.VMEM((2, 2, 128, wide), bf16),
            pltpu.VMEM((2, 2, 128, wide), bf16),
            pltpu.VMEM((2, 2, 8, wide), f32),
            pltpu.VMEM((TILES * 4, 128), f32),
            pltpu.VMEM((3, 256, 8, 128), f32),
            dma((2,)),
        ]
        + [dma((2, CHUNKS + 1))] * 6,
        compiler_params=pltpu.CompilerParams(vmem_limit_bytes=56 << 20, collective_id=0, has_side_effects=True),
    )(x, *(jnp.asarray(t) for t in tables()))


def relax_kernel(pieces, masks, carried, out, mine, blocks, result, sec_send, sec_recv, tile_send, tile_recv):
    sec, tile = lax.axis_index("sec"), lax.axis_index("tile")
    secs, tiles = lax.axis_size("sec"), lax.axis_size("tile")
    barrier = pltpu.get_barrier_semaphore()
    steps = (1, 2, tiles - 1, tiles - 2)
    slots = (1, 0, 3, 4)
    for k in range(1, secs):
        pl.semaphore_signal(barrier, inc=1, device_id=(lax.rem(sec + k, secs), tile), device_id_type=MESH)
    for k in steps:
        pl.semaphore_signal(barrier, inc=1, device_id=(sec, lax.rem(tile + k, tiles)), device_id_type=MESH)
    rows = [pieces[h, k] for h in range(2) for k in range(2)]
    rows += [masks[...].astype(f32), carried[0], carried[1], jnp.zeros((2, 128), f32)]
    mine[pl.ds(sec, 1)] = jnp.concatenate(rows, 0)[None]
    pl.semaphore_wait(barrier, secs - 1 + len(steps))

    def to_sec(k, owner):
        return pltpu.make_async_remote_copy(
            mine.at[owner],
            mine.at[owner],
            sec_send.at[k],
            sec_recv.at[k],
            device_id=(lax.rem(sec + k, secs), tile),
            device_id_type=MESH,
        )

    for k in range(1, secs):
        to_sec(k, sec).start()
    for k in range(1, secs):
        to_sec(k, lax.rem(sec + secs - k, secs)).wait_recv()
    for s in range(secs):
        whole = mine[0, 10:14] if s == 0 else mine[s, 0:4] + mine[s - 1, 4:8]
        blocks[2, s] = jnp.concatenate([whole, mine[s, 8:10], jnp.zeros((2, 128), f32)], 0)
    copies = [
        pltpu.make_async_remote_copy(
            blocks.at[2],
            blocks.at[slot],
            tile_send.at[n],
            tile_recv.at[n],
            device_id=(sec, lax.rem(tile + k, tiles)),
            device_id_type=MESH,
        )
        for n, (k, slot) in enumerate(zip(steps, slots))
    ]
    for copy in copies:
        copy.start()
    for copy in copies:
        copy.wait_recv()

    def window(get):
        return jnp.concatenate([get(0)[1:2], get(1), get(2), get(3), get(4)[0:1]], 0)

    flow = [[window(lambda d: blocks[d, s, 2 * k : 2 * k + 2]) for k in range(2)] for s in range(secs)]
    zero = jnp.zeros((8, 128), f32)
    pairs = [zero] + [link_weight * window(lambda d: blocks[d, s, 4:6]) for s in range(1, secs)] + [zero]
    node = 2 * tile - 3 + lax.broadcasted_iota(jnp.int32, (8, 128), 0)
    column = lax.broadcasted_iota(jnp.int32, (8, 128), 1)
    last = 2 * tiles - 1
    inside = jnp.logical_and(node >= 0, node <= last)
    at_left, at_right = column == 0, column == 127

    def as_float(test):
        return jnp.where(test, 1.0, 0.0)

    degree = 4.0 - as_float(node == 0) - as_float(node == last) - as_float(at_left) - as_float(at_right)
    start = [[jnp.where(inside, v, 0.0) for v in flow[0]]]
    for s in range(1, secs):
        start.append([start[s - 1][k] + jnp.where(inside, flow[s][k], 0.0) for k in range(2)])
    inverse = [
        jnp.where(inside, 1.0 / (spring_weight * degree + pairs[s] + pairs[s + 1] + anchor_weight), 0.0)
        for s in range(secs)
    ]
    fixed = []
    for s in range(secs):
        row = []
        for k in range(2):
            v = anchor_weight * start[s][k]
            if s > 0:
                v = v + pairs[s] * flow[s][k]
            if s + 1 < secs:
                v = v - pairs[s + 1] * flow[s + 1][k]
            row.append(v)
        fixed.append(row)
    aligned = start
    for step in range(ITERS):
        new = []
        for s in range(secs):
            row = []
            for k in range(2):
                v = aligned[s][k]
                total = fixed[s][k] + spring_weight * (
                    pltpu.roll(v, 1, 0)
                    + pltpu.roll(v, 7, 0)
                    + jnp.where(at_left, 0.0, pltpu.roll(v, 1, 1))
                    + jnp.where(at_right, 0.0, pltpu.roll(v, 127, 1))
                )
                if s > 0:
                    total = total + pairs[s] * aligned[s - 1][k]
                if s + 1 < secs:
                    total = total + pairs[s + 1] * aligned[s + 1][k]
                row.append(jnp.where(inside, total * inverse[s], 0.0))
            new.append(row)
        aligned = new
    for s in range(secs):
        for k in range(2):
            result[s, k] = flow[s][k]
            result[s, 2 + k] = aligned[s][k]
    for k in range(2):
        out[0, k] = result[sec, k][3:5]
        out[1, k] = result[sec, 2 + k][3:5]
    for k in range(1, secs):
        to_sec(k, sec).wait_send()
    for copy in copies:
        copy.wait_send()


def relaxed(pieces, masks, carried):
    vmem = pl.BlockSpec(memory_space=pltpu.VMEM)
    dma = pltpu.SemaphoreType.DMA
    secs = lax.axis_size("sec")
    return pl.pallas_call(
        relax_kernel,
        out_shape=jax.ShapeDtypeStruct((2, 2, 2, 128), f32),
        in_specs=[vmem] * 3,
        out_specs=vmem,
        scratch_shapes=[
            pltpu.VMEM((secs, 16, 128), f32),
            pltpu.VMEM((5, secs, 8, 128), f32),
            pltpu.VMEM((secs, 4, 8, 128), f32),
            dma((secs,)),
            dma((secs,)),
            dma((4,)),
            dma((4,)),
        ],
        compiler_params=pltpu.CompilerParams(collective_id=1, has_side_effects=True),
    )(pieces, masks, carried)


def shards(sections, masks, carried):
    both = relaxed(flow_of(sections[0]), masks[0], carried)
    return both[0:1], both[1:2]


def solution(mesh):
    in_specs = (P("sec", "tile", None), P("sec", "tile", None), P(None, "tile", None))
    out_specs = (P("sec", None, "tile", None), P("sec", None, "tile", None))
    return jax.shard_map(shards, mesh=mesh, in_specs=in_specs, out_specs=out_specs, check_vma=False)
```
